32 devices in a mesh: dom: 2 (over y), blk: 4 (over z), sub: 2 (over x), rep: 2 (over core).
Axes of the slice: x: 2, y: 2, z: 4, core: 2. Of those that a mesh axis runs over, the one named last changes fastest.
Arguments:
- tokens: bfloat16 [4096, 2048], P(('dom', 'blk', 'sub', 'rep')), parts along dimension 0, may hold values from -6 to 6
- expert_ids: int32 [4096, 8], P(('dom', 'blk', 'sub', 'rep')), parts along dimension 0, may hold values from 0 to 127, as said below
- gate_weights: float32 [4096, 8], P(('dom', 'blk', 'sub', 'rep')), parts along dimension 0, may hold values from 0.2 to 2
- w_gate: bfloat16 [2, 768, 2048], P('sub', 'rep', 'blk'), may hold values from -0.125 to 0.125
- w_up: bfloat16 [2, 768, 2048], P('sub', 'rep', 'blk'), may hold values from -0.125 to 0.125
- w_down: bfloat16 [2, 768, 2048], P('sub', 'rep', 'blk'), may hold values from -0.21875 to 0.21875
- cotangent: bfloat16 [4096, 2048], P(('dom', 'blk', 'sub', 'rep')), parts along dimension 0, may hold values from -6 to 6
Outputs:
- mixed: bfloat16 [4096, 2048], P(('dom', 'blk', 'sub', 'rep')), parts along dimension 0
- token_grad: bfloat16 [4096, 2048], P(('dom', 'blk', 'sub', 'rep')), parts along dimension 0
- gate_grad: float32 [4096, 8], P(('dom', 'blk', 'sub', 'rep')), parts along dimension 0
- grad_gate: float32 [4, 768, 2048], P(('dom', 'sub'), 'rep', 'blk'), parts along dimension 0
- grad_up: float32 [4, 768, 2048], P(('dom', 'sub'), 'rep', 'blk'), parts along dimension 0
- grad_down: float32 [4, 768, 2048], P(('dom', 'sub'), 'rep', 'blk'), parts along dimension 0
The draws below stay inside these ranges and needn't reach their ends.
There are 2 independent parts, one for each index of `dom`. The reference program is written for one: setup_inputs(seed, part) draws one part's arguments, and reference() takes and returns one part's arrays. A program takes and returns all parts, laid end to end along the dimension named above; an argument that names none is the same for every part. Nothing has to cross between parts.
Inputs may be any that keep to these rules, and one draw needn't show every extreme that they name: `expert_ids`: each row names 8 different experts. Among the 128 rows of one device, each expert below 2 is named by 1 to 12 rows, and in every draw some expert below 2 is named by 12 rows on every device of one blk index.
All inputs are finite; a program needn't handle non-finite values.
Results may differ from the reference program's by a relative error of at most 0.02.
Values may be sent and summed in bfloat16 or wider, within the bound.
A program may use at most 64 MiB of HBM per device.

```python
import math
import jax
import jax.numpy as jnp
from jax import lax

D = 2048
FF = 768
NUM_EXPERTS = 128
TOPK = 8
TOK_DEV = 128
CAP = 12
EXP_WIN = 2
LOOP_LEN = 4
SUB_LEN = 2
REP_LEN = 2
TOKENS = 2048


def draw_expert_ids(key, part):
    blocks = TOKENS // TOK_DEV
    key_count = jax.random.fold_in(key, 21)
    key_hot_blk = jax.random.fold_in(key, 22)
    key_hot_exp = jax.random.fold_in(key, 24)
    key_pick = jax.random.fold_in(key, 25)
    key_fill = jax.random.fold_in(key, 26)
    key_place = jax.random.fold_in(key, 27)
    counts = jax.random.randint(key_count, (LOOP_LEN, SUB_LEN, REP_LEN, EXP_WIN), 1, CAP + 1).astype(jnp.int32)
    hot_blk = jax.random.randint(key_hot_blk, (), 0, LOOP_LEN)
    hot_exp = jax.random.randint(key_hot_exp, (), 0, EXP_WIN)
    blk_iota = jnp.arange(LOOP_LEN, dtype=jnp.int32)[:, None, None, None]
    exp_iota = jnp.arange(EXP_WIN, dtype=jnp.int32)[None, None, None, :]
    full_group = (blk_iota == hot_blk) & (exp_iota == hot_exp)
    counts = jnp.where(full_group, CAP, counts).reshape(blocks, EXP_WIN)
    scores = jax.random.randint(key_pick, (blocks, EXP_WIN, TOK_DEV), 0, 1 << 20) * TOK_DEV + jnp.arange(TOK_DEV, dtype=jnp.int32)
    token_ranks = jnp.argsort(jnp.argsort(scores, axis=2), axis=2)
    chosen = token_ranks < counts[:, :, None]
    chosen = jnp.transpose(chosen, (0, 2, 1)).reshape(TOKENS, EXP_WIN)
    spare = NUM_EXPERTS - EXP_WIN
    fill_scores = jax.random.randint(key_fill, (TOKENS, spare), 0, 1 << 20) * NUM_EXPERTS + jnp.arange(spare, dtype=jnp.int32)
    chosen_ids = jnp.argsort(fill_scores, axis=1)[:, :TOPK].astype(jnp.int32) + EXP_WIN
    place_scores = jax.random.randint(key_place, (TOKENS, TOPK), 0, 1 << 20) * TOPK + jnp.arange(TOPK, dtype=jnp.int32)
    places = jnp.argsort(place_scores, axis=1).astype(jnp.int32)
    topk_iota = jnp.arange(TOPK, dtype=jnp.int32)[None, :]
    for expert in range(EXP_WIN):
        landing = (topk_iota == places[:, expert:expert + 1]) & chosen[:, expert:expert + 1]
        chosen_ids = jnp.where(landing, expert, chosen_ids)
    return chosen_ids.astype(jnp.int32)


def shard_levels(own_key, dims, split, smallest, high):
    level, own = 1.0, jax.random.fold_in(own_key, 6)
    for position, shards_of in split:
        draws = jnp.exp(jax.random.uniform(jax.random.fold_in(own, position), (shards_of,), jnp.float32, smallest / len(split), high / len(split)))
        level = level * jnp.repeat(draws, dims[position] // shards_of).reshape([-1 if axis == position else 1 for axis in range(len(dims))])
    return level


def scatter_about(key, shape, scale, reach, cuts=(), kind=jnp.bfloat16):
    values = jax.random.normal(key, shape, jnp.float32) * scale
    if len(cuts) > 0:
        values = shard_levels(key, shape, cuts, -0.22, 0.18) * values
    return jnp.clip(values, min=-reach, max=reach).astype(kind)


def setup_inputs(seed: int = 0, part: int = 0) -> dict:
    seeds = jax.random.split(jax.random.key(seed), 8)
    part_keys = jax.random.split(jax.random.fold_in(seeds[7], part), 8)
    tokens = scatter_about(part_keys[0], (TOKENS, D), 1.0, 6.0, ((0, 16),))
    expert_ids = draw_expert_ids(jax.random.fold_in(jax.random.fold_in(seeds[7], part), 71), part)
    gate_weights = jnp.clip(jnp.exp(math.log(2.0) - 2.3025851 * jax.random.uniform(part_keys[2], (TOKENS, TOPK), jnp.float32) ** shard_levels(part_keys[2], (TOKENS, TOPK), ((0, 16),), -0.2, 0.2)), 0.2, 2.0)
    w_gate = scatter_about(seeds[3], (EXP_WIN, FF, D), D ** -0.5, 0.125, ((0, 2), (1, 2), (2, 4)))
    w_up = scatter_about(seeds[4], (EXP_WIN, FF, D), D ** -0.5, 0.125, ((0, 2), (1, 2), (2, 4)))
    w_down = scatter_about(seeds[5], (EXP_WIN, FF, D), FF ** -0.5, 0.21875, ((0, 2), (1, 2), (2, 4)))
    cotangent = scatter_about(part_keys[6], (TOKENS, D), 1.0, 6.0, ((0, 16),))
    return {"tokens": tokens, "expert_ids": expert_ids, "gate_weights": gate_weights, "w_gate": w_gate, "w_up": w_up, "w_down": w_down, "cotangent": cotangent}


def silu_pair(pre_act):
    sigmoid_v = jax.nn.sigmoid(pre_act)
    return (pre_act * sigmoid_v, sigmoid_v * (1.0 + pre_act * (1.0 - sigmoid_v)))

def slot_table(expert_ids, expert):
    blocks = TOKENS // TOK_DEV
    named_hits = expert_ids == expert
    picked = lax.optimization_barrier(jnp.sum(named_hits.astype(jnp.int32), axis=1)).astype(jnp.int32).reshape(blocks, TOK_DEV)
    before = (jnp.cumsum(picked, axis=1).astype(jnp.int32) - picked).astype(jnp.int32)
    slot_iota = jnp.arange(CAP, dtype=jnp.int32)
    placed = (before[:, None, :] == slot_iota[None, :, None]) & (picked[:, None, :] > 0)
    local_iota = jnp.arange(TOK_DEV, dtype=jnp.int32)
    local_row = lax.optimization_barrier(jnp.sum(jnp.where(placed, local_iota[None, None, :], 0), axis=2)).astype(jnp.int32)
    offsets = (jnp.arange(blocks, dtype=jnp.int32) * TOK_DEV)[:, None]
    row_index = (local_row + offsets).reshape(-1).astype(jnp.int32)
    valid_row = jnp.any(placed, axis=2).reshape(-1)
    return (named_hits, row_index, valid_row)

def half_sum(left_a, right_a, left_b, right_b):
    slice_len = FF // REP_LEN
    result = jnp.zeros((left_a.shape[0], D), jnp.float32)
    for block in range(REP_LEN):
        lower = block * slice_len
        partial_value = jnp.dot(left_a[:, lower:lower + slice_len], right_a[lower:lower + slice_len], preferred_element_type=jnp.float32)
        if left_b is not None:
            partial_value = partial_value + jnp.dot(left_b[:, lower:lower + slice_len], right_b[lower:lower + slice_len], preferred_element_type=jnp.float32)
        result = result + lax.optimization_barrier(partial_value.astype(jnp.bfloat16)).astype(jnp.float32)
    return lax.optimization_barrier(result.astype(jnp.bfloat16)).astype(jnp.float32)

def group_grad(left, right, grad_scale):
    left_rows = left.astype(jnp.float32).reshape(LOOP_LEN, -1, left.shape[1])
    right_rows = right.astype(jnp.float32).reshape(LOOP_LEN, -1, right.shape[1])
    parts = jnp.einsum('brf,brd->bfd', left_rows, right_rows, precision=lax.Precision.HIGHEST) * grad_scale
    return lax.optimization_barrier(jnp.sum(lax.optimization_barrier(parts.astype(jnp.bfloat16)).astype(jnp.float32), axis=0))

def reference(tokens, expert_ids, gate_weights, w_gate, w_up, w_down, cotangent):
    grad_scale = (TOKENS * TOPK / NUM_EXPERTS) ** (-0.5)
    mixed_sum = jnp.zeros((TOKENS, D), jnp.float32)
    input_sum = jnp.zeros((TOKENS, D), jnp.float32)
    gate_grad = jnp.zeros((TOKENS, TOPK), jnp.float32)
    grads_gate = []
    grads_up = []
    grads_down = []
    for expert in range(EXP_WIN):
        named_hits, row_index, valid_row = slot_table(expert_ids, expert)
        weight_of = lax.optimization_barrier(jnp.sum(jnp.where(named_hits, gate_weights, jnp.zeros((), jnp.float32)), axis=1))
        row_weight = jnp.where(valid_row, weight_of[row_index], jnp.zeros((), jnp.float32))
        row_tokens = jnp.where(valid_row[:, None], tokens[row_index], jnp.zeros((), jnp.bfloat16))
        row_cotan = jnp.where(valid_row[:, None], cotangent[row_index], jnp.zeros((), jnp.bfloat16))
        pre_gate = jnp.dot(row_tokens, w_gate[expert].T, preferred_element_type=jnp.float32)
        pre_up = jnp.dot(row_tokens, w_up[expert].T, preferred_element_type=jnp.float32)
        activated, silu_slope = silu_pair(pre_gate)
        hidden = (activated * pre_up).astype(jnp.bfloat16)
        expert_out = half_sum(hidden, w_down[expert], None, None)
        mixed_sum = mixed_sum.at[row_index].add(row_weight[:, None] * expert_out)
        row_dot = lax.optimization_barrier(jnp.sum(row_cotan.astype(jnp.float32) * expert_out, axis=1))
        token_dot = jnp.zeros((TOKENS,), jnp.float32).at[row_index].add(jnp.where(valid_row, row_dot, jnp.zeros((), jnp.float32)))
        gate_grad = gate_grad + jnp.where(named_hits, token_dot[:, None], jnp.zeros((), jnp.float32))
        row_dout = (row_weight[:, None] * row_cotan.astype(jnp.float32)).astype(jnp.bfloat16)
        dhidden = jnp.dot(row_dout, w_down[expert].T, preferred_element_type=jnp.float32)
        dpre_gate = (dhidden * pre_up * silu_slope).astype(jnp.bfloat16)
        dpre_up = (dhidden * activated).astype(jnp.bfloat16)
        input_rows = half_sum(dpre_gate, w_gate[expert], dpre_up, w_up[expert])
        input_sum = input_sum.at[row_index].add(input_rows)
        grads_gate.append(group_grad(dpre_gate, row_tokens, grad_scale))
        grads_up.append(group_grad(dpre_up, row_tokens, grad_scale))
        grads_down.append(group_grad(hidden, row_dout, grad_scale))
    return (mixed_sum.astype(jnp.bfloat16), input_sum.astype(jnp.bfloat16), gate_grad, jnp.stack(grads_gate), jnp.stack(grads_up), jnp.stack(grads_down))
```

```python
import functools

import jax
import jax.numpy as jnp
from jax import lax
from jax.experimental import pallas as pl
from jax.experimental.pallas import tpu as pltpu
from jax.sharding import PartitionSpec as P

NUM_EXPERTS = 128
TOPK = 8
CAP = 12
MESH = pl.DeviceIdType.MESH
BF16 = jnp.bfloat16
F32 = jnp.float32


def each(low, high, body):
    if high - low <= 8:
        for i in range(low, high):
            body(i)
    else:

        def step(i, carry):
            body(i)
            return carry

        lax.fori_loop(low, high, step, 0)


def div_mod(k, n):
    if isinstance(k, int):
        return k // n, k % n
    return lax.div(k, n), lax.rem(k, n)


def steps_of(v, width, count):
    out = jnp.zeros_like(v)
    for m in range(1, count):
        out = out + (v >= m * width).astype(jnp.int32)
    return out


def dot(a, b):
    return jnp.dot(a, b, preferred_element_type=F32)


def dot_nt(a, b):
    return lax.dot_general(a, b, (((1,), (1,)), ((), ())), preferred_element_type=F32)


def dot_tn(a, b):
    return lax.dot_general(a, b, (((0,), (0,)), ((), ())), preferred_element_type=F32)


def as_mask(cond):
    return jnp.where(cond, 1.0, 0.0).astype(BF16)


def kernel(
    dims,
    ids_ref,
    gw_ref,
    tok_ref,
    cot_ref,
    wg_ref,
    wu_ref,
    wd_ref,
    mixed_ref,
    tgrad_ref,
    ggrad_ref,
    gg_ref,
    gu_ref,
    gd_ref,
    mt_ref,
    wt_ref,
    send1,
    recv1,
    cots,
    xs,
    dos,
    part_own,
    part_send,
    part_recv,
    hid,
    px_own,
    px_send,
    px_recv,
    fin,
    back,
    disp_s,
    disp_r,
    fwd_s,
    fwd_r,
    rs_s,
    rs_r,
    ag_s,
    ag_r,
    px_s,
    px_r,
    bk_s,
    bk_r,
):
    n_blk, n_sub, n_rep, halves, pack, scale = dims
    tok_count = tok_ref.shape[0]
    d_blk = wg_ref.shape[2]
    ff = wg_ref.shape[1]
    width = d_blk // halves
    per_blk = n_sub * n_rep
    chunk = per_blk * CAP
    rows = n_sub * pack
    lanes = mt_ref.shape[1]
    kinds = 2 * halves
    b = lax.axis_index("blk")
    s = lax.axis_index("sub")
    r = lax.axis_index("rep")
    other = 1 - r

    def wrap(v, n):
        return lax.rem(v + n, n)

    barrier = pltpu.get_barrier_semaphore()
    group = n_blk * n_sub * n_rep

    def greet(k):
        db, rest = div_mod(k, n_sub * n_rep)
        ds, dr = div_mod(rest, n_rep)
        pl.semaphore_signal(
            barrier,
            inc=1,
            device_id={"blk": wrap(b + db, n_blk), "sub": wrap(s + ds, n_sub), "rep": wrap(r + dr, n_rep)},
            device_id_type=MESH,
        )

    each(1, group, greet)

    lane = lax.broadcasted_iota(jnp.int32, (tok_count, lanes), 1)
    lane_exp = steps_of(lane, pack, n_sub)
    lane_in = lane - lane_exp * pack
    lane_kind = steps_of(lane_in, CAP, kinds + 1)
    lane_slot = lane_in - lane_kind * CAP
    picked = jnp.zeros((tok_count, lanes), F32)
    weight = jnp.zeros((tok_count, lanes), F32)
    for k in range(ids_ref.shape[1]):
        hit = ids_ref[:, k : k + 1] == lane_exp
        picked = picked + jnp.where(hit, 1.0, 0.0)
        weight = weight + jnp.where(hit, gw_ref[:, k : k + 1], 0.0)
    row_i = lax.broadcasted_iota(jnp.int32, (tok_count, tok_count), 0)
    col_i = lax.broadcasted_iota(jnp.int32, (tok_count, tok_count), 1)
    before = dot(as_mask(col_i < row_i), picked.astype(BF16))
    live = (lane_kind < kinds) & (lane < rows)
    placed = (before == lane_slot.astype(F32)) & (picked > 0.0) & live
    mt = jnp.where(placed, 1.0, 0.0)
    wt = jnp.where(placed, weight, 0.0)
    mt_ref[...] = mt
    wt_ref[...] = wt
    sel = mt.T[:rows]
    slot_gate = jnp.sum(wt.T[:rows], axis=1, keepdims=True)
    sub_i = lax.broadcasted_iota(jnp.int32, (rows, 1), 0)
    sub_exp = steps_of(sub_i, pack, n_sub)
    sub_kind = steps_of(sub_i - sub_exp * pack, CAP, kinds + 1)
    is_cot = sub_kind == 1
    for h in range(1, halves):
        is_cot = is_cot | (sub_kind == 2 * h + 1)
    row_scale = jnp.where(is_cot, slot_gate, 1.0)
    takes = [jnp.where(sub_kind == x, sel, 0.0).astype(BF16) for x in range(kinds)]

    def columns(blk, h):
        return pl.ds(pl.multiple_of(blk * d_blk + h * width, width), width)

    my_q = b * per_blk + r * n_sub + s

    def disp_copy(k):
        db, ds = div_mod(k, n_sub)
        dst_b, dst_s = wrap(b + db, n_blk), wrap(s + ds, n_sub)
        return pltpu.make_async_remote_copy(
            src_ref=send1.at[dst_b, dst_s],
            dst_ref=recv1.at[my_q],
            send_sem=disp_s.at[k],
            recv_sem=disp_r.at[k],
            device_id={"blk": dst_b, "sub": dst_s},
            device_id_type=MESH,
        )

    def fwd_copy(k):
        db, ds = div_mod(k, n_sub)
        q = wrap(b - db, n_blk) * per_blk + r * n_sub + wrap(s - ds, n_sub)
        return pltpu.make_async_remote_copy(
            src_ref=recv1.at[q],
            dst_ref=recv1.at[q],
            send_sem=fwd_s.at[k],
            recv_sem=fwd_r.at[k],
            device_id={"rep": other},
            device_id_type=MESH,
        )

    def gather(db):
        blk = wrap(b + db, n_blk)
        acc = None
        for h in range(halves):
            cols = columns(blk, h)
            term = dot(takes[2 * h], tok_ref[:, cols]) + dot(takes[2 * h + 1], cot_ref[:, cols])
            acc = term if acc is None else acc + term
        send1[blk] = (acc * row_scale).astype(BF16).reshape(n_sub, pack, width)

    def send_rows(db):
        each(0, n_sub, lambda ds: disp_copy(db * n_sub + ds).start())

    gather(1)
    pl.semaphore_wait(barrier, group - 1)
    send_rows(1)

    def gather_send(db):
        gather(db)
        send_rows(db)

    each(2, n_blk, gather_send)
    gather(0)
    each(1, n_sub, lambda ds: disp_copy(ds).start())
    recv1[my_q] = send1[b, s]
    fwd_copy(0).start()

    def forward(db):
        def one(ds):
            k = db * n_sub + ds
            disp_copy(k).wait_recv()
            fwd_copy(k).start()

        each(0, n_sub, one)

    def forward_first(ds):
        disp_copy(ds).wait_recv()
        fwd_copy(ds).start()

    each(1, n_sub, forward_first)

    prow = lax.broadcasted_iota(jnp.int32, (chunk, per_blk * pack), 0)
    pcol = lax.broadcasted_iota(jnp.int32, (chunk, per_blk * pack), 1)
    prow_g = steps_of(prow, CAP, per_blk)
    pcol_g = steps_of(pcol, pack, per_blk)
    prow_c = prow - prow_g * CAP
    pcol_j = pcol - pcol_g * pack
    unpack = [as_mask((prow_g == pcol_g) & (pcol_j == x * CAP + prow_c)) for x in range(kinds)]

    def cot_rows(db):
        blk = wrap(b + db, n_blk)
        acc = None
        for h in range(halves):
            term = dot(takes[2 * h], cot_ref[:, columns(blk, h)])
            acc = term if acc is None else acc + term
        cots[blk] = acc.astype(BF16)

    each(0, n_blk, cot_rows)

    def rs_copy(db):
        return pltpu.make_async_remote_copy(
            src_ref=part_send.at[db],
            dst_ref=part_recv.at[db],
            send_sem=rs_s.at[db],
            recv_sem=rs_r.at[db],
            device_id={"blk": wrap(b - db, n_blk)},
            device_id_type=MESH,
        )

    def partial(db):
        blk = wrap(b - db, n_blk)
        each(0, n_sub, lambda ds: fwd_copy(db * n_sub + ds).wait_recv())
        block = recv1[pl.ds(blk * per_blk, per_blk)].reshape(per_blk * pack, width)
        for h in range(halves):
            xs[blk, :, h * width : (h + 1) * width] = dot(unpack[2 * h], block).astype(BF16)
            dos[blk, :, h * width : (h + 1) * width] = dot(unpack[2 * h + 1], block).astype(BF16)
        x, do = xs[blk], dos[blk]
        return dot_nt(x, wg_ref[0]), dot_nt(x, wu_ref[0]), dot_nt(do, wd_ref[0])

    def partial_send(db):
        for m, value in enumerate(partial(db)):
            part_send[db, :, m * ff : (m + 1) * ff] = value.astype(BF16)
        rs_copy(db).start()

    forward(1)
    for m, value in enumerate(partial(0)):
        part_own[:, m * ff : (m + 1) * ff] = value

    def middle(db):
        forward(db + 1)
        partial_send(db)

    each(1, n_blk - 1, middle)
    partial_send(n_blk - 1)

    def add_part(db):
        rs_copy(db).wait_recv()
        part_own[...] += part_recv[db].astype(F32)

    each(1, n_blk, add_part)
    pre_gate = part_own[:, :ff]
    pre_up = part_own[:, ff : 2 * ff]
    dhid = part_own[:, 2 * ff :]
    sig = jax.nn.sigmoid(pre_gate)
    act = pre_gate * sig
    slope = sig * (1.0 + pre_gate * (1.0 - sig))
    hid[b, :, :ff] = (act * pre_up).astype(BF16)
    hid[b, :, ff : 2 * ff] = (dhid * pre_up * slope).astype(BF16)
    hid[b, :, 2 * ff :] = (dhid * act).astype(BF16)

    def ag_copy(db):
        return pltpu.make_async_remote_copy(
            src_ref=hid.at[b],
            dst_ref=hid.at[b],
            send_sem=ag_s.at[db],
            recv_sem=ag_r.at[db],
            device_id={"blk": wrap(b + db, n_blk)},
            device_id_type=MESH,
        )

    each(1, n_blk, lambda db: ag_copy(db).start())

    srow = lax.broadcasted_iota(jnp.int32, (rows, chunk), 0)
    scol = lax.broadcasted_iota(jnp.int32, (rows, chunk), 1)
    srow_s = steps_of(srow, pack, n_sub)
    srow_j = srow - srow_s * pack
    srow_x = steps_of(srow_j, CAP, kinds + 1)
    srow_at = srow_s * CAP + srow_j - srow_x * CAP

    def repack(rep):
        at = scol == srow_at + rep * (n_sub * CAP)
        return [as_mask(at & (srow_x == x)) for x in range(kinds)]

    to_mine, to_other = repack(r), repack(other)

    def px_copy(db):
        return pltpu.make_async_remote_copy(
            src_ref=px_send.at[db],
            dst_ref=px_recv.at[db],
            send_sem=px_s.at[db],
            recv_sem=px_r.at[db],
            device_id={"rep": other},
            device_id_type=MESH,
        )

    def bk_copy(k):
        db, ds = div_mod(k, n_sub)
        dst_s = wrap(s + ds, n_sub)
        return pltpu.make_async_remote_copy(
            src_ref=fin.at[db, dst_s],
            dst_ref=back.at[b, s],
            send_sem=bk_s.at[k],
            recv_sem=bk_r.at[k],
            device_id={"blk": wrap(b - db, n_blk), "sub": dst_s},
            device_id_type=MESH,
        )

    def outputs(db):
        blk = wrap(b - db, n_blk)
        out = dot(hid[blk, :, :ff], wd_ref[0]).astype(BF16)
        into = dot(hid[blk, :, ff : 2 * ff], wg_ref[0]) + dot(hid[blk, :, 2 * ff :], wu_ref[0])
        into = into.astype(BF16)

        def packed(masks):
            acc = None
            for h in range(halves):
                cols = slice(h * width, (h + 1) * width)
                term = dot(masks[2 * h], out[:, cols]) + dot(masks[2 * h + 1], into[:, cols])
                acc = term if acc is None else acc + term
            return acc.astype(BF16).reshape(n_sub, pack, width)

        px_send[db] = packed(to_other)
        px_copy(db).start()
        px_own[db] = packed(to_mine)

    def finish(db):
        px_copy(db).wait_recv()
        fin[db] = (px_own[db].astype(F32) + px_recv[db].astype(F32)).astype(BF16)

    outputs(0)

    def rest(db):
        ag_copy(db).wait_recv()
        outputs(db)
        finish(db)
        each(0, n_sub, lambda ds: bk_copy(db * n_sub + ds).start())

    each(1, n_blk, rest)
    finish(0)
    each(1, n_sub, lambda ds: bk_copy(ds).start())
    back[b, s] = fin[0, s]

    x_all = xs[...].reshape(n_blk * chunk, d_blk)
    do_all = dos[...].reshape(n_blk * chunk, d_blk)
    gd_ref[0] = dot_tn(hid[:, :, :ff].reshape(n_blk * chunk, ff), do_all) * scale
    gg_ref[0] = dot_tn(hid[:, :, ff : 2 * ff].reshape(n_blk * chunk, ff), x_all) * scale
    gu_ref[0] = dot_tn(hid[:, :, 2 * ff :].reshape(n_blk * chunk, ff), x_all) * scale

    wt_all = wt_ref[:, :rows]
    wt_high = wt_all.astype(BF16)
    wt_low = (wt_all - wt_high.astype(F32)).astype(BF16)
    mt_low = mt_ref[:, :rows].astype(BF16)
    kind_row = lane_kind[:, :rows]
    none = jnp.zeros((tok_count, rows), BF16)

    def collect(db, dots):
        blk = wrap(b + db, n_blk)
        got = back[blk].reshape(rows, width)
        for h in range(halves):
            cols = columns(blk, h)
            high = jnp.where(kind_row == 2 * h, wt_high, none)
            low = jnp.where(kind_row == 2 * h, wt_low, none)
            ones = jnp.where(kind_row == 2 * h + 1, mt_low, none)
            mixed_ref[:, cols] = (dot(high, got) + dot(low, got)).astype(BF16)
            tgrad_ref[:, cols] = dot(ones, got).astype(BF16)
        return dots + jnp.sum(cots[blk].astype(F32) * got.astype(F32), axis=1, keepdims=True)

    each(1, n_sub, lambda ds: bk_copy(ds).wait_recv())
    dots = collect(0, jnp.zeros((rows, 1), F32))

    def step(db, dots):
        each(0, n_sub, lambda ds: bk_copy(db * n_sub + ds).wait_recv())
        return collect(db, dots)

    if n_blk <= 8:
        for db in range(1, n_blk):
            dots = step(db, dots)
    else:
        dots = lax.fori_loop(1, n_blk, step, dots)
    wide = jnp.broadcast_to(dots, (rows, tok_count))
    if lanes > rows:
        wide = jnp.concatenate([wide, jnp.zeros((lanes - rows, tok_count), F32)], axis=0)
    token_dots = mt_ref[...] * wide.T
    picks = []
    for k in range(ids_ref.shape[1]):
        hit = ids_ref[:, k : k + 1] == lane_exp
        picks.append(jnp.sum(jnp.where(hit, token_dots, 0.0), axis=1, keepdims=True))
    ggrad_ref[...] = jnp.concatenate(picks, axis=1)

    each(1, n_blk * n_sub, lambda k: disp_copy(k).wait_send())
    each(0, n_blk * n_sub, lambda k: fwd_copy(k).wait_send())
    each(1, n_blk, lambda db: rs_copy(db).wait_send())
    each(1, n_blk, lambda db: ag_copy(db).wait_send())
    each(0, n_blk, lambda db: px_copy(db).wait_send())
    each(1, n_blk * n_sub, lambda k: bk_copy(k).wait_send())


def on_device(tokens, expert_ids, gate_weights, w_gate, w_up, w_down, cotangent):
    n_blk, n_sub, n_rep = (lax.axis_size(name) for name in ("blk", "sub", "rep"))
    tok_count, d_model = tokens.shape
    _, ff, d_blk = w_gate.shape
    scale = (tok_count * n_blk * n_sub * n_rep * TOPK / NUM_EXPERTS) ** (-0.5)
    halves = 2 if d_blk % 256 == 0 else 1
    width = d_blk // halves
    pack = -(-2 * halves * CAP // 16) * 16
    rows = n_sub * pack
    lanes = -(-rows // 128) * 128
    chunk = n_sub * n_rep * CAP
    pairs = n_blk * n_sub
    dma = pltpu.SemaphoreType.DMA
    vmem = pl.BlockSpec(memory_space=pltpu.VMEM)
    dims = (n_blk, n_sub, n_rep, halves, pack, scale)
    grad = jax.ShapeDtypeStruct((1, ff, d_blk), F32)
    return pl.pallas_call(
        functools.partial(kernel, dims),
        out_shape=(
            jax.ShapeDtypeStruct((tok_count, d_model), BF16),
            jax.ShapeDtypeStruct((tok_count, d_model), BF16),
            jax.ShapeDtypeStruct(gate_weights.shape, F32),
            grad,
            grad,
            grad,
        ),
        in_specs=[vmem] * 7,
        out_specs=(vmem,) * 6,
        scratch_shapes=[
            pltpu.VMEM((tok_count, lanes), F32),
            pltpu.VMEM((tok_count, lanes), F32),
            pltpu.VMEM((n_blk, n_sub, pack, width), BF16),
            pltpu.VMEM((pairs * n_rep, pack, width), BF16),
            pltpu.VMEM((n_blk, rows, width), BF16),
            pltpu.VMEM((n_blk, chunk, d_blk), BF16),
            pltpu.VMEM((n_blk, chunk, d_blk), BF16),
            pltpu.VMEM((chunk, 3 * ff), F32),
            pltpu.VMEM((n_blk, chunk, 3 * ff), BF16),
            pltpu.VMEM((n_blk, chunk, 3 * ff), BF16),
            pltpu.VMEM((n_blk, chunk, 3 * ff), BF16),
            pltpu.VMEM((n_blk, n_sub, pack, width), BF16),
            pltpu.VMEM((n_blk, n_sub, pack, width), BF16),
            pltpu.VMEM((n_blk, n_sub, pack, width), BF16),
            pltpu.VMEM((n_blk, n_sub, pack, width), BF16),
            pltpu.VMEM((n_blk, n_sub, pack, width), BF16),
            dma((pairs,)),
            dma((pairs,)),
            dma((pairs,)),
            dma((pairs,)),
            dma((n_blk,)),
            dma((n_blk,)),
            dma((n_blk,)),
            dma((n_blk,)),
            dma((n_blk,)),
            dma((n_blk,)),
            dma((pairs,)),
            dma((pairs,)),
        ],
        compiler_params=pltpu.CompilerParams(
            collective_id=0, has_side_effects=True, vmem_limit_bytes=56 * 1024 * 1024
        ),
        cost_estimate=pl.CostEstimate(flops=1 << 30, bytes_accessed=8 << 20, transcendentals=chunk * ff),
    )(expert_ids, gate_weights, tokens, cotangent, w_gate, w_up, w_down)


def solution(mesh):
    rows = P(("dom", "blk", "sub", "rep"), None)
    weights = P("sub", "rep", "blk")
    grads = P(("dom", "sub"), "rep", "blk")
    return jax.shard_map(
        on_device,
        mesh=mesh,
        in_specs=(rows, rows, rows, weights, weights, weights, rows),
        out_specs=(rows, rows, rows, grads, grads, grads),
        check_vma=False,
    )
```

```python
import functools
import math

import jax
import jax.numpy as jnp
from jax import lax
from jax.experimental import pallas as pl
from jax.experimental.pallas import tpu as pltpu
from jax.sharding import PartitionSpec as P

NUM_EXPERTS = 128
TOPK = 8
CAP = 12
MESH = pl.DeviceIdType.MESH
BF16 = jnp.bfloat16
F32 = jnp.float32


def each(low, high, body):
    if high - low <= 8:
        for i in range(low, high):
            body(i)
    else:

        def step(i, carry):
            body(i)
            return carry

        lax.fori_loop(low, high, step, 0)


def div_mod(k, n):
    if isinstance(k, int):
        return k // n, k % n
    return lax.div(k, n), lax.rem(k, n)


def steps_of(v, width, count):
    out = jnp.zeros_like(v)
    for m in range(1, count):
        out = out + (v >= m * width).astype(jnp.int32)
    return out


def dot(a, b):
    return jnp.dot(a, b, preferred_element_type=F32)


def dot_nt(a, b):
    return lax.dot_general(a, b, (((1,), (1,)), ((), ())), preferred_element_type=F32)


def dot_tn(a, b):
    return lax.dot_general(a, b, (((0,), (0,)), ((), ())), preferred_element_type=F32)


def as_mask(cond):
    return jnp.where(cond, 1.0, 0.0).astype(BF16)


def kernel(
    dims,
    ids_ref,
    gw_ref,
    tok_ref,
    cot_ref,
    wg_hbm,
    wu_hbm,
    wd_hbm,
    sel_ref,
    selw_ref,
    cots,
    xs,
    dos,
    hid,
    back,
    wg_ref,
    wu_ref,
    wd_ref,
    send1,
    recv1,
    part_own,
    part_send,
    part_recv,
    px_own,
    px_send,
    px_recv,
    fin,
    w_s,
    disp_s,
    disp_r,
    fwd_s,
    fwd_r,
    rs_s,
    rs_r,
    ag_s,
    ag_r,
    px_s,
    px_r,
    bk_s,
    bk_r,
):
    n_blk, n_sub, n_rep, halves, pack = dims
    tok_count = tok_ref.shape[0]
    d_blk = wg_ref.shape[2]
    ff = wg_ref.shape[1]
    width = d_blk // halves
    per_blk = n_sub * n_rep
    chunk = per_blk * CAP
    rows = n_sub * pack
    kinds = 2 * halves
    b = lax.axis_index("blk")
    s = lax.axis_index("sub")
    r = lax.axis_index("rep")
    other = 1 - r

    def wrap(v, n):
        return lax.rem(v + n, n)

    fetches = [
        pltpu.make_async_copy(src, dst, w_s.at[i])
        for i, (src, dst) in enumerate(((wg_hbm, wg_ref), (wu_hbm, wu_ref), (wd_hbm, wd_ref)))
    ]
    for fetch in fetches:
        fetch.start()

    barrier = pltpu.get_barrier_semaphore()
    group = n_blk * n_sub * n_rep

    def greet(k):
        db, rest = div_mod(k, n_sub * n_rep)
        ds, dr = div_mod(rest, n_rep)
        pl.semaphore_signal(
            barrier,
            inc=1,
            device_id={"blk": wrap(b + db, n_blk), "sub": wrap(s + ds, n_sub), "rep": wrap(r + dr, n_rep)},
            device_id_type=MESH,
        )

    each(1, group, greet)

    sub_i = lax.broadcasted_iota(jnp.int32, (rows, tok_count), 0)
    sub_exp = steps_of(sub_i, pack, n_sub)
    sub_in = sub_i - sub_exp * pack
    sub_kind = steps_of(sub_in, CAP, kinds + 1)
    sub_slot = sub_in - sub_kind * CAP
    picked = jnp.zeros((rows, tok_count), F32)
    weight = jnp.zeros((rows, tok_count), F32)
    for k in range(ids_ref.shape[0]):
        hit = ids_ref[k : k + 1, :] == sub_exp
        picked = picked + jnp.where(hit, 1.0, 0.0)
        weight = weight + jnp.where(hit, gw_ref[k : k + 1, :], 0.0)
    row_i = lax.broadcasted_iota(jnp.int32, (tok_count, tok_count), 0)
    col_i = lax.broadcasted_iota(jnp.int32, (tok_count, tok_count), 1)
    before = dot(picked.astype(BF16), as_mask(row_i < col_i))
    placed = (before == sub_slot.astype(F32)) & (picked > 0.0) & (sub_kind < kinds)
    sel = jnp.where(placed, 1.0, 0.0)
    selw = jnp.where(placed, weight, 0.0)
    sel_ref[...] = sel
    selw_ref[...] = selw
    slot_gate = jnp.sum(selw, axis=1, keepdims=True)
    is_cot = sub_kind == 1
    for h in range(1, halves):
        is_cot = is_cot | (sub_kind == 2 * h + 1)
    row_scale = jnp.where(is_cot, jnp.broadcast_to(slot_gate, is_cot.shape), 1.0)[:, :1]
    takes = [jnp.where(sub_kind == x, sel, 0.0).astype(BF16) for x in range(kinds)]

    def columns(blk, h):
        return pl.ds(pl.multiple_of(blk * d_blk + h * width, width), width)

    my_q = b * per_blk + r * n_sub + s

    def disp_copy(k):
        db, ds = div_mod(k, n_sub)
        dst_b, dst_s = wrap(b + db, n_blk), wrap(s + ds, n_sub)
        return pltpu.make_async_remote_copy(
            src_ref=send1.at[dst_b, dst_s],
            dst_ref=recv1.at[my_q],
            send_sem=disp_s.at[k],
            recv_sem=disp_r.at[k],
            device_id={"blk": dst_b, "sub": dst_s},
            device_id_type=MESH,
        )

    def fwd_copy(k):
        db, ds = div_mod(k, n_sub)
        q = wrap(b - db, n_blk) * per_blk + r * n_sub + wrap(s - ds, n_sub)
        return pltpu.make_async_remote_copy(
            src_ref=recv1.at[q],
            dst_ref=recv1.at[q],
            send_sem=fwd_s.at[k],
            recv_sem=fwd_r.at[k],
            device_id={"rep": other},
            device_id_type=MESH,
        )

    def gather(db):
        blk = wrap(b + db, n_blk)
        acc = None
        for h in range(halves):
            cols = columns(blk, h)
            term = dot(takes[2 * h], tok_ref[:, cols]) + dot(takes[2 * h + 1], cot_ref[:, cols])
            acc = term if acc is None else acc + term
        send1[blk] = (acc * row_scale).astype(BF16).reshape(n_sub, pack, width)

    def send_rows(db):
        each(0, n_sub, lambda ds: disp_copy(db * n_sub + ds).start())

    gather(1)
    pl.semaphore_wait(barrier, group - 1)
    send_rows(1)

    def gather_send(db):
        gather(db)
        send_rows(db)

    each(2, n_blk, gather_send)
    gather(0)
    each(1, n_sub, lambda ds: disp_copy(ds).start())
    recv1[my_q] = send1[b, s]
    fwd_copy(0).start()

    def forward(db):
        def one(ds):
            k = db * n_sub + ds
            disp_copy(k).wait_recv()
            fwd_copy(k).start()

        each(0, n_sub, one)

    def forward_first(ds):
        disp_copy(ds).wait_recv()
        fwd_copy(ds).start()

    each(1, n_sub, forward_first)

    prow = lax.broadcasted_iota(jnp.int32, (chunk, per_blk * pack), 0)
    pcol = lax.broadcasted_iota(jnp.int32, (chunk, per_blk * pack), 1)
    prow_g = steps_of(prow, CAP, per_blk)
    pcol_g = steps_of(pcol, pack, per_blk)
    prow_c = prow - prow_g * CAP
    pcol_j = pcol - pcol_g * pack
    unpack = [as_mask((prow_g == pcol_g) & (pcol_j == x * CAP + prow_c)) for x in range(kinds)]

    def cot_rows(db):
        blk = wrap(b + db, n_blk)
        acc = None
        for h in range(halves):
            term = dot(takes[2 * h], cot_ref[:, columns(blk, h)])
            acc = term if acc is None else acc + term
        cots[blk] = acc.astype(BF16)

    each(0, n_blk, cot_rows)

    def rs_copy(db):
        return pltpu.make_async_remote_copy(
            src_ref=part_send.at[db],
            dst_ref=part_recv.at[db],
            send_sem=rs_s.at[db],
            recv_sem=rs_r.at[db],
            device_id={"blk": wrap(b - db, n_blk)},
            device_id_type=MESH,
        )

    def partial(db):
        blk = wrap(b - db, n_blk)
        each(0, n_sub, lambda ds: fwd_copy(db * n_sub + ds).wait_recv())
        block = recv1[pl.ds(blk * per_blk, per_blk)].reshape(per_blk * pack, width)
        for h in range(halves):
            xs[blk, :, h * width : (h + 1) * width] = dot(unpack[2 * h], block).astype(BF16)
            dos[blk, :, h * width : (h + 1) * width] = dot(unpack[2 * h + 1], block).astype(BF16)
        x, do = xs[blk], dos[blk]
        return dot_nt(x, wg_ref[0]), dot_nt(x, wu_ref[0]), dot_nt(do, wd_ref[0])

    def partial_send(db):
        for m, value in enumerate(partial(db)):
            part_send[db, :, m * ff : (m + 1) * ff] = value.astype(BF16)
        rs_copy(db).start()

    for fetch in fetches:
        fetch.wait()
    forward(1)
    for m, value in enumerate(partial(0)):
        part_own[:, m * ff : (m + 1) * ff] = value

    def middle(db):
        forward(db + 1)
        partial_send(db)

    each(1, n_blk - 1, middle)
    partial_send(n_blk - 1)

    def add_part(db):
        rs_copy(db).wait_recv()
        part_own[...] += part_recv[db].astype(F32)

    each(1, n_blk, add_part)
    pre_gate = part_own[:, :ff]
    pre_up = part_own[:, ff : 2 * ff]
    dhid = part_own[:, 2 * ff :]
    sig = jax.nn.sigmoid(pre_gate)
    act = pre_gate * sig
    slope = sig * (1.0 + pre_gate * (1.0 - sig))
    hid[b, :, :ff] = (act * pre_up).astype(BF16)
    hid[b, :, ff : 2 * ff] = (dhid * pre_up * slope).astype(BF16)
    hid[b, :, 2 * ff :] = (dhid * act).astype(BF16)

    def ag_copy(db):
        return pltpu.make_async_remote_copy(
            src_ref=hid.at[b],
            dst_ref=hid.at[b],
            send_sem=ag_s.at[db],
            recv_sem=ag_r.at[db],
            device_id={"blk": wrap(b + db, n_blk)},
            device_id_type=MESH,
        )

    each(1, n_blk, lambda db: ag_copy(db).start())

    srow = lax.broadcasted_iota(jnp.int32, (rows, chunk), 0)
    scol = lax.broadcasted_iota(jnp.int32, (rows, chunk), 1)
    srow_s = steps_of(srow, pack, n_sub)
    srow_j = srow - srow_s * pack
    srow_x = steps_of(srow_j, CAP, kinds + 1)
    srow_at = srow_s * CAP + srow_j - srow_x * CAP

    def repack(rep):
        at = scol == srow_at + rep * (n_sub * CAP)
        return [as_mask(at & (srow_x == x)) for x in range(kinds)]

    to_mine, to_other = repack(r), repack(other)

    def px_copy(db):
        return pltpu.make_async_remote_copy(
            src_ref=px_send.at[db],
            dst_ref=px_recv.at[db],
            send_sem=px_s.at[db],
            recv_sem=px_r.at[db],
            device_id={"rep": other},
            device_id_type=MESH,
        )

    def bk_copy(k):
        db, ds = div_mod(k, n_sub)
        dst_s = wrap(s + ds, n_sub)
        return pltpu.make_async_remote_copy(
            src_ref=fin.at[db, dst_s],
            dst_ref=back.at[b, s],
            send_sem=bk_s.at[k],
            recv_sem=bk_r.at[k],
            device_id={"blk": wrap(b - db, n_blk), "sub": dst_s},
            device_id_type=MESH,
        )

    def outputs(db):
        blk = wrap(b - db, n_blk)
        out = dot(hid[blk, :, :ff], wd_ref[0]).astype(BF16)
        into = dot(hid[blk, :, ff : 2 * ff], wg_ref[0]) + dot(hid[blk, :, 2 * ff :], wu_ref[0])
        into = into.astype(BF16)

        def packed(masks):
            acc = None
            for h in range(halves):
                cols = slice(h * width, (h + 1) * width)
                term = dot(masks[2 * h], out[:, cols]) + dot(masks[2 * h + 1], into[:, cols])
                acc = term if acc is None else acc + term
            return acc.astype(BF16).reshape(n_sub, pack, width)

        px_send[db] = packed(to_other)
        px_copy(db).start()
        px_own[db] = packed(to_mine)

    def finish(db):
        px_copy(db).wait_recv()
        fin[db] = (px_own[db].astype(F32) + px_recv[db].astype(F32)).astype(BF16)

    outputs(0)

    def rest(db):
        ag_copy(db).wait_recv()
        outputs(db)
        finish(db)
        each(0, n_sub, lambda ds: bk_copy(db * n_sub + ds).start())

    each(1, n_blk, rest)
    finish(0)
    each(1, n_sub, lambda ds: bk_copy(ds).start())
    back[b, s] = fin[0, s]

    each(1, n_blk * n_sub, lambda k: bk_copy(k).wait_recv())

    each(1, n_blk * n_sub, lambda k: disp_copy(k).wait_send())
    each(0, n_blk * n_sub, lambda k: fwd_copy(k).wait_send())
    each(1, n_blk, lambda db: rs_copy(db).wait_send())
    each(1, n_blk, lambda db: ag_copy(db).wait_send())
    each(0, n_blk, lambda db: px_copy(db).wait_send())
    each(1, n_blk * n_sub, lambda k: bk_copy(k).wait_send())


def finish_kernel(
    dims,
    ids_ref,
    sel_ref,
    selw_ref,
    cots,
    xs,
    dos,
    hid,
    back,
    mixed_hbm,
    tgrad_hbm,
    ggrad_hbm,
    gg_hbm,
    gu_hbm,
    gd_hbm,
    mixed_ref,
    tgrad_ref,
    ggrad_ref,
    gg_ref,
    gu_ref,
    gd_ref,
    sems,
):
    n_blk, n_sub, halves, pack, scale = dims
    d_blk = xs.shape[2]
    all_rows = n_blk * xs.shape[1]
    ff = hid.shape[2] // 3
    width = d_blk // halves
    rows = n_sub * pack
    kinds = 2 * halves
    pairs = (
        (mixed_ref, mixed_hbm),
        (tgrad_ref, tgrad_hbm),
        (ggrad_ref, ggrad_hbm),
        (gg_ref, gg_hbm),
        (gu_ref, gu_hbm),
        (gd_ref, gd_hbm),
    )
    outs = [pltpu.make_async_copy(src, dst, sems.at[i]) for i, (src, dst) in enumerate(pairs)]
    x_all = xs[...].reshape(all_rows, d_blk)
    gg_ref[0] = dot_tn(hid[:, :, ff : 2 * ff].reshape(all_rows, ff), x_all) * scale
    outs[3].start()
    gu_ref[0] = dot_tn(hid[:, :, 2 * ff :].reshape(all_rows, ff), x_all) * scale
    outs[4].start()
    do_all = dos[...].reshape(all_rows, d_blk)
    gd_ref[0] = dot_tn(hid[:, :, :ff].reshape(all_rows, ff), do_all) * scale
    outs[5].start()

    tok_count = sel_ref.shape[1]
    sub_i = lax.broadcasted_iota(jnp.int32, (rows, tok_count), 0)
    sub_exp = steps_of(sub_i, pack, n_sub)
    sub_kind = steps_of(sub_i - sub_exp * pack, CAP, kinds + 1)
    selw = selw_ref[...]
    high = selw.astype(BF16).astype(F32)
    low = selw - high
    takes = []
    for h in range(halves):
        mine = sub_kind == 2 * h
        takes.append(
            [
                jnp.where(mine, high, 0.0).T.astype(BF16),
                jnp.where(mine, low, 0.0).T.astype(BF16),
                jnp.where(sub_kind == 2 * h + 1, sel_ref[...], 0.0).T.astype(BF16),
            ]
        )
    dots = jnp.zeros((rows, 1), F32)
    for blk in range(n_blk):
        got = back[blk].reshape(rows, width)
        for h in range(halves):
            cols = slice(blk * d_blk + h * width, blk * d_blk + (h + 1) * width)
            high_t, low_t, ones_t = takes[h]
            mixed_ref[:, cols] = (dot(high_t, got) + dot(low_t, got)).astype(BF16)
            tgrad_ref[:, cols] = dot(ones_t, got).astype(BF16)
        dots = dots + jnp.sum(cots[blk].astype(F32) * got.astype(F32), axis=1, keepdims=True)
    outs[0].start()
    outs[1].start()
    token_dots = sel_ref[...] * dots
    for k in range(ids_ref.shape[0]):
        hit = ids_ref[k : k + 1, :] == sub_exp
        ggrad_ref[k : k + 1, :] = jnp.sum(jnp.where(hit, token_dots, 0.0), axis=0, keepdims=True)
    outs[2].start()
    for out in outs:
        out.wait()


def on_device(tokens, expert_ids, gate_weights, w_gate, w_up, w_down, cotangent):
    n_blk, n_sub, n_rep = (lax.axis_size(name) for name in ("blk", "sub", "rep"))
    tok_count, d_model = tokens.shape
    _, ff, d_blk = w_gate.shape
    scale = (tok_count * n_blk * n_sub * n_rep * TOPK / NUM_EXPERTS) ** (-0.5)
    halves = 2 if d_blk % 256 == 0 else 1
    width = d_blk // halves
    pack = -(-2 * halves * CAP // 16) * 16
    rows = n_sub * pack
    chunk = n_sub * n_rep * CAP
    pairs = n_blk * n_sub
    dma = pltpu.SemaphoreType.DMA
    vmem = pl.BlockSpec(memory_space=pltpu.VMEM)
    anywhere = pl.BlockSpec(memory_space=pl.ANY)
    packed = (n_blk, n_sub, pack, width)
    shaped = jax.ShapeDtypeStruct
    handed = (
        shaped((rows, tok_count), F32),
        shaped((rows, tok_count), F32),
        shaped((n_blk, rows, width), BF16),
        shaped((n_blk, chunk, d_blk), BF16),
        shaped((n_blk, chunk, d_blk), BF16),
        shaped((n_blk, chunk, 3 * ff), BF16),
        shaped(packed, BF16),
    )
    held = [
        ((1, ff, d_blk), BF16),
        ((1, ff, d_blk), BF16),
        ((1, ff, d_blk), BF16),
        (packed, BF16),
        ((pairs * n_rep, pack, width), BF16),
        ((chunk, 3 * ff), F32),
        ((n_blk, chunk, 3 * ff), BF16),
        ((n_blk, chunk, 3 * ff), BF16),
        (packed, BF16),
        (packed, BF16),
        (packed, BF16),
        (packed, BF16),
    ]
    inside = sum(math.prod(shape) * jnp.dtype(kind).itemsize for shape, kind in held)
    inside += sum(math.prod(one.shape) * one.dtype.itemsize for one in handed)
    ids, gates = expert_ids.T, gate_weights.T
    between = pl.pallas_call(
        functools.partial(kernel, (n_blk, n_sub, n_rep, halves, pack)),
        out_shape=handed,
        in_specs=[vmem] * 4 + [anywhere] * 3,
        out_specs=(vmem,) * len(handed),
        scratch_shapes=[pltpu.VMEM(shape, kind) for shape, kind in held]
        + [dma((3,))]
        + [dma((pairs,))] * 4
        + [dma((n_blk,))] * 6
        + [dma((pairs,))] * 2,
        compiler_params=pltpu.CompilerParams(
            collective_id=0,
            has_side_effects=True,
            vmem_limit_bytes=(12 << 20) + inside + inside // 4,
        ),
        cost_estimate=pl.CostEstimate(flops=1 << 30, bytes_accessed=8 << 20, transcendentals=chunk * ff),
    )(ids, gates, tokens, cotangent, w_gate, w_up, w_down)
    grad = shaped((1, ff, d_blk), F32)
    results = (
        shaped((tok_count, d_model), BF16),
        shaped((tok_count, d_model), BF16),
        shaped(gates.shape, F32),
        grad,
        grad,
        grad,
    )
    room = sum(math.prod(one.shape) * one.dtype.itemsize for one in handed + results)
    mixed, token_grad, gate_grad, grad_gate, grad_up, grad_down = pl.pallas_call(
        functools.partial(finish_kernel, (n_blk, n_sub, halves, pack, scale)),
        out_shape=results,
        in_specs=[vmem] * (1 + len(handed)),
        out_specs=(anywhere,) * len(results),
        scratch_shapes=[pltpu.VMEM(one.shape, one.dtype) for one in results] + [dma((len(results),))],
        compiler_params=pltpu.CompilerParams(vmem_limit_bytes=(12 << 20) + room + room // 4),
        cost_estimate=pl.CostEstimate(flops=1 << 28, bytes_accessed=5 << 20, transcendentals=0),
    )(ids, *between)
    return mixed, token_grad, gate_grad.T, grad_gate, grad_up, grad_down


def solution(mesh):
    rows = P(("dom", "blk", "sub", "rep"), None)
    weights = P("sub", "rep", "blk")
    grads = P(("dom", "sub"), "rep", "blk")
    return jax.shard_map(
        on_device,
        mesh=mesh,
        in_specs=(rows, rows, rows, weights, weights, weights, rows),
        out_specs=(rows, rows, rows, grads, grads, grads),
        check_vma=False,
    )
```

```python
import functools

import jax
import jax.numpy as jnp
from jax import lax
from jax.experimental import pallas as pl
from jax.experimental.pallas import tpu as pltpu
from jax.sharding import PartitionSpec as P

NUM_EXPERTS = 128
TOPK = 8
CAP = 12
VMEM_LIMIT = 60 << 20
MESH = pl.DeviceIdType.MESH
BF16 = jnp.bfloat16
F32 = jnp.float32


def each(low, high, body):
    if high - low <= 8:
        for i in range(low, high):
            body(i)
    else:

        def step(i, carry):
            body(i)
            return carry

        lax.fori_loop(low, high, step, 0)


def div_mod(k, n):
    if isinstance(k, int):
        return k // n, k % n
    return lax.div(k, n), lax.rem(k, n)


def steps_of(v, width, count):
    out = jnp.zeros_like(v)
    for m in range(1, count):
        out = out + (v >= m * width).astype(jnp.int32)
    return out


def dot(a, b):
    return jnp.dot(a, b, preferred_element_type=F32)


def dot_nt(a, b):
    return lax.dot_general(a, b, (((1,), (1,)), ((), ())), preferred_element_type=F32)


def dot_tn(a, b):
    return lax.dot_general(a, b, (((0,), (0,)), ((), ())), preferred_element_type=F32)


def as_mask(cond):
    return jnp.where(cond, 1.0, 0.0).astype(BF16)


def kernel(
    dims,
    ids_hbm,
    gw_hbm,
    tok_hbm,
    cot_hbm,
    wg_hbm,
    wu_hbm,
    wd_hbm,
    ids_ref,
    sel_ref,
    selw_ref,
    cots,
    xs,
    dos,
    hid,
    back,
    gw_ref,
    tok_ref,
    cot_ref,
    wg_ref,
    wu_ref,
    wd_ref,
    send1,
    recv1,
    part_own,
    part_send,
    part_recv,
    px_own,
    px_send,
    px_recv,
    fin,
    in_s,
    disp_s,
    disp_r,
    fwd_s,
    fwd_r,
    rs_s,
    rs_r,
    ag_s,
    ag_r,
    ag_l,
    px_s,
    px_r,
    bk_s,
    bk_r,
):
    n_blk, n_sub, n_rep, halves, pack = dims
    tok_count = tok_ref.shape[0]
    d_blk = wg_ref.shape[2]
    ff = wg_ref.shape[1]
    width = d_blk // halves
    per_blk = n_sub * n_rep
    chunk = per_blk * CAP
    rows = n_sub * pack
    kinds = 2 * halves
    pieces = hid.shape[1]
    unit = ff // pieces
    b = lax.axis_index("blk")
    s = lax.axis_index("sub")
    r = lax.axis_index("rep")
    other = 1 - r

    def wrap(v, n):
        return lax.rem(v + n, n)

    operands = (
        (ids_hbm, ids_ref),
        (gw_hbm, gw_ref),
        (tok_hbm, tok_ref),
        (cot_hbm, cot_ref),
        (wg_hbm, wg_ref),
        (wu_hbm, wu_ref),
        (wd_hbm, wd_ref),
    )
    fetches = [pltpu.make_async_copy(src, dst, in_s.at[i]) for i, (src, dst) in enumerate(operands)]
    for fetch in fetches:
        fetch.start()

    barrier = pltpu.get_barrier_semaphore()
    group = n_blk * n_sub * n_rep

    def greet(k):
        db, rest = div_mod(k, n_sub * n_rep)
        ds, dr = div_mod(rest, n_rep)
        pl.semaphore_signal(
            barrier,
            inc=1,
            device_id={"blk": wrap(b + db, n_blk), "sub": wrap(s + ds, n_sub), "rep": wrap(r + dr, n_rep)},
            device_id_type=MESH,
        )

    each(1, group, greet)

    for fetch in fetches[:2]:
        fetch.wait()

    sub_i = lax.broadcasted_iota(jnp.int32, (rows, tok_count), 0)
    sub_exp = steps_of(sub_i, pack, n_sub)
    sub_in = sub_i - sub_exp * pack
    sub_kind = steps_of(sub_in, CAP, kinds + 1)
    sub_slot = sub_in - sub_kind * CAP
    picked = jnp.zeros((rows, tok_count), F32)
    weight = jnp.zeros((rows, tok_count), F32)
    for k in range(ids_ref.shape[0]):
        hit = ids_ref[k : k + 1, :] == sub_exp
        picked = picked + jnp.where(hit, 1.0, 0.0)
        weight = weight + jnp.where(hit, gw_ref[k : k + 1, :], 0.0)
    row_i = lax.broadcasted_iota(jnp.int32, (tok_count, tok_count), 0)
    col_i = lax.broadcasted_iota(jnp.int32, (tok_count, tok_count), 1)
    before = dot(picked.astype(BF16), as_mask(row_i < col_i))
    placed = (before == sub_slot.astype(F32)) & (picked > 0.0) & (sub_kind < kinds)
    sel = jnp.where(placed, 1.0, 0.0)
    selw = jnp.where(placed, weight, 0.0)
    sel_ref[...] = sel
    selw_ref[...] = selw
    slot_gate = jnp.sum(selw, axis=1, keepdims=True)
    is_cot = sub_kind == 1
    for h in range(1, halves):
        is_cot = is_cot | (sub_kind == 2 * h + 1)
    row_scale = jnp.where(is_cot, jnp.broadcast_to(slot_gate, is_cot.shape), 1.0)[:, :1]
    takes = [jnp.where(sub_kind == x, sel, 0.0).astype(BF16) for x in range(kinds)]

    def columns(blk, h):
        return pl.ds(pl.multiple_of(blk * d_blk + h * width, width), width)

    my_q = b * per_blk + r * n_sub + s

    def disp_copy(k):
        db, ds = div_mod(k, n_sub)
        dst_b, dst_s = wrap(b + db, n_blk), wrap(s + ds, n_sub)
        return pltpu.make_async_remote_copy(
            src_ref=send1.at[dst_b, dst_s],
            dst_ref=recv1.at[my_q],
            send_sem=disp_s.at[k],
            recv_sem=disp_r.at[k],
            device_id={"blk": dst_b, "sub": dst_s},
            device_id_type=MESH,
        )

    def fwd_copy(k):
        db, ds = div_mod(k, n_sub)
        q = wrap(b - db, n_blk) * per_blk + r * n_sub + wrap(s - ds, n_sub)
        return pltpu.make_async_remote_copy(
            src_ref=recv1.at[q],
            dst_ref=recv1.at[q],
            send_sem=fwd_s.at[k],
            recv_sem=fwd_r.at[k],
            device_id={"rep": other},
            device_id_type=MESH,
        )

    def gather(db):
        blk = wrap(b + db, n_blk)
        acc = None
        for h in range(halves):
            cols = columns(blk, h)
            term = dot(takes[2 * h], tok_ref[:, cols]) + dot(takes[2 * h + 1], cot_ref[:, cols])
            acc = term if acc is None else acc + term
        send1[blk] = (acc * row_scale).astype(BF16).reshape(n_sub, pack, width)

    def send_rows(db):
        each(0, n_sub, lambda ds: disp_copy(db * n_sub + ds).start())

    for fetch in fetches[2:4]:
        fetch.wait()
    gather(1)
    pl.semaphore_wait(barrier, group - 1)
    send_rows(1)

    def gather_send(db):
        gather(db)
        send_rows(db)

    each(2, n_blk, gather_send)
    gather(0)
    each(1, n_sub, lambda ds: disp_copy(ds).start())
    recv1[my_q] = send1[b, s]
    fwd_copy(0).start()

    def forward(db):
        def one(ds):
            k = db * n_sub + ds
            disp_copy(k).wait_recv()
            fwd_copy(k).start()

        each(0, n_sub, one)

    def forward_first(ds):
        disp_copy(ds).wait_recv()
        fwd_copy(ds).start()

    each(1, n_sub, forward_first)

    prow = lax.broadcasted_iota(jnp.int32, (chunk, per_blk * pack), 0)
    pcol = lax.broadcasted_iota(jnp.int32, (chunk, per_blk * pack), 1)
    prow_g = steps_of(prow, CAP, per_blk)
    pcol_g = steps_of(pcol, pack, per_blk)
    prow_c = prow - prow_g * CAP
    pcol_j = pcol - pcol_g * pack
    unpack = [as_mask((prow_g == pcol_g) & (pcol_j == x * CAP + prow_c)) for x in range(kinds)]

    def cot_rows(db):
        blk = wrap(b + db, n_blk)
        acc = None
        for h in range(halves):
            term = dot(takes[2 * h], cot_ref[:, columns(blk, h)])
            acc = term if acc is None else acc + term
        cots[blk] = acc.astype(BF16)

    each(0, n_blk, cot_rows)

    def rs_copy(db, p):
        return pltpu.make_async_remote_copy(
            src_ref=part_send.at[db, p],
            dst_ref=part_recv.at[db, p],
            send_sem=rs_s.at[db * pieces + p],
            recv_sem=rs_r.at[db * pieces + p],
            device_id={"blk": wrap(b - db, n_blk)},
            device_id_type=MESH,
        )

    def partial(db):
        blk = wrap(b - db, n_blk)
        each(0, n_sub, lambda ds: fwd_copy(db * n_sub + ds).wait_recv())
        block = recv1[pl.ds(blk * per_blk, per_blk)].reshape(per_blk * pack, width)
        for h in range(halves):
            xs[blk, :, h * width : (h + 1) * width] = dot(unpack[2 * h], block).astype(BF16)
            dos[blk, :, h * width : (h + 1) * width] = dot(unpack[2 * h + 1], block).astype(BF16)
        x, do = xs[blk], dos[blk]
        return dot_nt(x, wg_ref[0]), dot_nt(x, wu_ref[0]), dot_nt(do, wd_ref[0])

    def partial_send(db):
        values = partial(db)
        for p in range(pieces):
            for m, value in enumerate(values):
                part_send[db, p, :, m * unit : (m + 1) * unit] = value[:, p * unit : (p + 1) * unit].astype(BF16)
            rs_copy(db, p).start()

    for fetch in fetches[4:]:
        fetch.wait()
    forward(1)
    for m, value in enumerate(partial(0)):
        for p in range(pieces):
            part_own[p, :, m * unit : (m + 1) * unit] = value[:, p * unit : (p + 1) * unit]

    def middle(db):
        forward(db + 1)
        partial_send(db)

    each(1, n_blk - 1, middle)
    partial_send(n_blk - 1)

    def ag_copy(c, p, to, sem):
        return pltpu.make_async_remote_copy(
            src_ref=hid.at[c, p],
            dst_ref=hid.at[c, p],
            send_sem=sem,
            recv_sem=ag_r.at[c * pieces + p],
            device_id={"blk": to},
            device_id_type=MESH,
        )

    def to_right(p):
        return ag_copy(b, p, wrap(b + 1, n_blk), ag_s.at[b * pieces + p])

    def to_left(p):
        return ag_copy(b, p, wrap(b - 1, n_blk), ag_l.at[p])

    def both_ways(p, act):
        @pl.when(b + 1 < n_blk)
        def _():
            act(to_right(p))

        @pl.when(b >= 1)
        def _():
            act(to_left(p))

    for p in range(pieces):

        def add_part(db):
            rs_copy(db, p).wait_recv()
            part_own[p] += part_recv[db, p].astype(F32)

        each(1, n_blk, add_part)
        pre_gate = part_own[p, :, :unit]
        pre_up = part_own[p, :, unit : 2 * unit]
        dhid = part_own[p, :, 2 * unit :]
        sig = jax.nn.sigmoid(pre_gate)
        act = pre_gate * sig
        slope = sig * (1.0 + pre_gate * (1.0 - sig))
        hid[b, p, :, :unit] = (act * pre_up).astype(BF16)
        hid[b, p, :, unit : 2 * unit] = (dhid * pre_up * slope).astype(BF16)
        hid[b, p, :, 2 * unit :] = (dhid * act).astype(BF16)
        both_ways(p, lambda copy: copy.start())

    def pass_copy(c, p, step):
        return ag_copy(c, p, wrap(b + step, n_blk), ag_s.at[c * pieces + p])

    def take(c, step):
        for p in range(pieces):
            pass_copy(c, p, step).wait_recv()

            @pl.when((b + step >= 0) & (b + step < n_blk))
            def _():
                pass_copy(c, p, step).start()

    def passed(c, step):
        for p in range(pieces):

            @pl.when((b + step >= 0) & (b + step < n_blk))
            def _():
                pass_copy(c, p, step).wait_send()

    def at_distance(d, fn):
        @pl.when(b - d >= 0)
        def _():
            fn(b - d, 1)

        @pl.when(b + d < n_blk)
        def _():
            fn(b + d, -1)

    srow = lax.broadcasted_iota(jnp.int32, (rows, chunk), 0)
    scol = lax.broadcasted_iota(jnp.int32, (rows, chunk), 1)
    srow_s = steps_of(srow, pack, n_sub)
    srow_j = srow - srow_s * pack
    srow_x = steps_of(srow_j, CAP, kinds + 1)
    srow_at = srow_s * CAP + srow_j - srow_x * CAP

    def repack(rep):
        at = scol == srow_at + rep * (n_sub * CAP)
        return [as_mask(at & (srow_x == x)) for x in range(kinds)]

    to_mine, to_other = repack(r), repack(other)

    def px_copy(c):
        return pltpu.make_async_remote_copy(
            src_ref=px_send.at[c],
            dst_ref=px_recv.at[c],
            send_sem=px_s.at[c],
            recv_sem=px_r.at[c],
            device_id={"rep": other},
            device_id_type=MESH,
        )

    def bk_copy(c, dst_s):
        return pltpu.make_async_remote_copy(
            src_ref=fin.at[c, dst_s],
            dst_ref=back.at[b, s],
            send_sem=bk_s.at[c * n_sub + dst_s],
            recv_sem=bk_r.at[b * n_sub + s],
            device_id={"blk": c, "sub": dst_s},
            device_id_type=MESH,
        )

    def bk_arrival(k):
        db, ds = div_mod(k, n_sub)
        from_b, from_s = wrap(b + db, n_blk), wrap(s + ds, n_sub)
        return pltpu.make_async_remote_copy(
            src_ref=fin.at[from_b, from_s],
            dst_ref=back.at[from_b, from_s],
            send_sem=bk_s.at[from_b * n_sub + from_s],
            recv_sem=bk_r.at[from_b * n_sub + from_s],
            device_id={"blk": from_b, "sub": from_s},
            device_id_type=MESH,
        )

    def outputs(c, step):
        def whole(m):
            return jnp.concatenate([hid[c, p, :, m * unit : (m + 1) * unit] for p in range(pieces)], axis=1)

        out = dot(whole(0), wd_ref[0]).astype(BF16)
        into = (dot(whole(1), wg_ref[0]) + dot(whole(2), wu_ref[0])).astype(BF16)

        def packed(masks):
            acc = None
            for h in range(halves):
                cols = slice(h * width, (h + 1) * width)
                term = dot(masks[2 * h], out[:, cols]) + dot(masks[2 * h + 1], into[:, cols])
                acc = term if acc is None else acc + term
            return acc.astype(BF16).reshape(n_sub, pack, width)

        px_send[c] = packed(to_other)
        px_copy(c).start()
        px_own[c] = packed(to_mine)

    def finish(c, step):
        px_copy(c).wait_recv()
        fin[c] = (px_own[c].astype(F32) + px_recv[c].astype(F32)).astype(BF16)
        each(0, n_sub, lambda dst_s: bk_copy(c, dst_s).start())

    outputs(b, 0)

    def rest(d):
        at_distance(d, take)
        at_distance(d, outputs)
        at_distance(d, finish)

    each(1, n_blk, rest)
    px_copy(b).wait_recv()
    fin[b] = (px_own[b].astype(F32) + px_recv[b].astype(F32)).astype(BF16)
    each(1, n_sub, lambda ds: bk_copy(b, wrap(s + ds, n_sub)).start())
    back[b, s] = fin[b, s]
    each(1, n_blk * n_sub, lambda k: bk_arrival(k).wait_recv())

    each(1, n_blk * n_sub, lambda k: disp_copy(k).wait_send())
    each(0, n_blk * n_sub, lambda k: fwd_copy(k).wait_send())
    for p in range(pieces):
        each(1, n_blk, lambda db: rs_copy(db, p).wait_send())
        both_ways(p, lambda copy: copy.wait_send())
    each(1, n_blk, lambda d: at_distance(d, passed))
    each(0, n_blk, lambda c: px_copy(c).wait_send())
    each(1, n_blk * n_sub, lambda k: bk_arrival(k).wait_send())


def finish_kernel(
    dims,
    ids_hbm,
    sel_hbm,
    selw_hbm,
    cots_hbm,
    xs_hbm,
    dos_hbm,
    hid_hbm,
    back_hbm,
    mixed_hbm,
    tgrad_hbm,
    ggrad_hbm,
    gg_hbm,
    gu_hbm,
    gd_hbm,
    mixed_ref,
    tgrad_ref,
    ggrad_ref,
    gg_ref,
    gu_ref,
    gd_ref,
    ids_ref,
    sel_ref,
    selw_ref,
    cots,
    xs,
    dos,
    hid,
    back,
    sems,
    in_sems,
):
    n_blk, n_sub, halves, pack, scale = dims
    d_blk = xs.shape[2]
    all_rows = n_blk * xs.shape[1]
    pieces, unit = hid.shape[1], hid.shape[3] // 3
    width = d_blk // halves
    rows = n_sub * pack
    kinds = 2 * halves
    pairs = (
        (mixed_ref, mixed_hbm),
        (tgrad_ref, tgrad_hbm),
        (ggrad_ref, ggrad_hbm),
        (gg_ref, gg_hbm),
        (gu_ref, gu_hbm),
        (gd_ref, gd_hbm),
    )
    outs = [pltpu.make_async_copy(src, dst, sems.at[i]) for i, (src, dst) in enumerate(pairs)]
    operands = (
        (xs_hbm, xs),
        (hid_hbm, hid),
        (dos_hbm, dos),
        (ids_hbm, ids_ref),
        (sel_hbm, sel_ref),
        (selw_hbm, selw_ref),
        (cots_hbm, cots),
        (back_hbm, back),
    )
    fetches = [pltpu.make_async_copy(src, dst, in_sems.at[i]) for i, (src, dst) in enumerate(operands)]
    for fetch in fetches:
        fetch.start()
    for fetch in fetches[:3]:
        fetch.wait()
    x_all = xs[...].reshape(all_rows, d_blk)
    do_all = dos[...].reshape(all_rows, d_blk)

    def weight_grad(m, right, out_ref):
        for p in range(pieces):
            left = hid[:, p, :, m * unit : (m + 1) * unit].reshape(all_rows, unit)
            out_ref[0, p * unit : (p + 1) * unit, :] = dot_tn(left, right) * scale

    weight_grad(1, x_all, gg_ref)
    outs[3].start()
    weight_grad(2, x_all, gu_ref)
    outs[4].start()
    weight_grad(0, do_all, gd_ref)
    outs[5].start()

    for fetch in fetches[3:]:
        fetch.wait()
    tok_count = sel_ref.shape[1]
    sub_i = lax.broadcasted_iota(jnp.int32, (rows, tok_count), 0)
    sub_exp = steps_of(sub_i, pack, n_sub)
    sub_kind = steps_of(sub_i - sub_exp * pack, CAP, kinds + 1)
    selw = selw_ref[...]
    high = selw.astype(BF16).astype(F32)
    low = selw - high
    takes = []
    for h in range(halves):
        mine = sub_kind == 2 * h
        takes.append(
            [
                jnp.where(mine, high, 0.0).T.astype(BF16),
                jnp.where(mine, low, 0.0).T.astype(BF16),
                jnp.where(sub_kind == 2 * h + 1, sel_ref[...], 0.0).T.astype(BF16),
            ]
        )
    dots = jnp.zeros((rows, 1), F32)
    for blk in range(n_blk):
        got = back[blk].reshape(rows, width)
        for h in range(halves):
            cols = slice(blk * d_blk + h * width, blk * d_blk + (h + 1) * width)
            high_t, low_t, ones_t = takes[h]
            mixed_ref[:, cols] = (dot(high_t, got) + dot(low_t, got)).astype(BF16)
            tgrad_ref[:, cols] = dot(ones_t, got).astype(BF16)
        dots = dots + jnp.sum(cots[blk].astype(F32) * got.astype(F32), axis=1, keepdims=True)
    outs[0].start()
    outs[1].start()
    token_dots = sel_ref[...] * dots
    for k in range(ids_ref.shape[0]):
        hit = ids_ref[k : k + 1, :] == sub_exp
        ggrad_ref[k : k + 1, :] = jnp.sum(jnp.where(hit, token_dots, 0.0), axis=0, keepdims=True)
    outs[2].start()
    for out in outs:
        out.wait()


def on_device(tokens, expert_ids, gate_weights, w_gate, w_up, w_down, cotangent):
    n_blk, n_sub, n_rep = (lax.axis_size(name) for name in ("blk", "sub", "rep"))
    tok_count, d_model = tokens.shape
    _, ff, d_blk = w_gate.shape
    scale = (tok_count * n_blk * n_sub * n_rep * TOPK / NUM_EXPERTS) ** (-0.5)
    halves = 2 if d_blk % 256 == 0 else 1
    width = d_blk // halves
    pack = -(-2 * halves * CAP // 16) * 16
    rows = n_sub * pack
    chunk = n_sub * n_rep * CAP
    pairs = n_blk * n_sub
    dma = pltpu.SemaphoreType.DMA
    vmem = pl.BlockSpec(memory_space=pltpu.VMEM)
    anywhere = pl.BlockSpec(memory_space=pl.ANY)
    packed = (n_blk, n_sub, pack, width)
    shaped = jax.ShapeDtypeStruct
    pieces = ff // 128 if ff % 128 == 0 else 1
    spread = (n_blk, pieces, chunk, 3 * ff // pieces)
    ids, gates = expert_ids.T, gate_weights.T
    handed = (
        shaped(ids.shape, ids.dtype),
        shaped((rows, tok_count), F32),
        shaped((rows, tok_count), F32),
        shaped((n_blk, rows, width), BF16),
        shaped((n_blk, chunk, d_blk), BF16),
        shaped((n_blk, chunk, d_blk), BF16),
        shaped(spread, BF16),
        shaped(packed, BF16),
    )
    held = [
        (gates.shape, F32),
        (tokens.shape, BF16),
        (tokens.shape, BF16),
        ((1, ff, d_blk), BF16),
        ((1, ff, d_blk), BF16),
        ((1, ff, d_blk), BF16),
        (packed, BF16),
        ((pairs * n_rep, pack, width), BF16),
        (spread[1:], F32),
        (spread, BF16),
        (spread, BF16),
        (packed, BF16),
        (packed, BF16),
        (packed, BF16),
        (packed, BF16),
    ]
    between = pl.pallas_call(
        functools.partial(kernel, (n_blk, n_sub, n_rep, halves, pack)),
        out_shape=handed,
        in_specs=[pl.BlockSpec(memory_space=pltpu.HBM)] * 7,
        out_specs=(vmem,) * len(handed),
        scratch_shapes=[pltpu.VMEM(shape, kind) for shape, kind in held]
        + [dma((7,))]
        + [dma((pairs,))] * 4
        + [dma((n_blk * pieces,))] * 4
        + [dma((pieces,))]
        + [dma((n_blk,))] * 2
        + [dma((pairs,))] * 2,
        compiler_params=pltpu.CompilerParams(
            collective_id=0,
            has_side_effects=True,
            vmem_limit_bytes=VMEM_LIMIT,
        ),
        cost_estimate=pl.CostEstimate(flops=1 << 30, bytes_accessed=8 << 20, transcendentals=chunk * ff),
    )(ids, gates, tokens, cotangent, w_gate, w_up, w_down)
    grad = shaped((1, ff, d_blk), F32)
    results = (
        shaped((tok_count, d_model), BF16),
        shaped((tok_count, d_model), BF16),
        shaped(gates.shape, F32),
        grad,
        grad,
        grad,
    )
    mixed, token_grad, gate_grad, grad_gate, grad_up, grad_down = pl.pallas_call(
        functools.partial(finish_kernel, (n_blk, n_sub, halves, pack, scale)),
        out_shape=results,
        in_specs=[anywhere] * len(handed),
        out_specs=(anywhere,) * len(results),
        scratch_shapes=[pltpu.VMEM(one.shape, one.dtype) for one in results + handed]
        + [dma((len(results),)), dma((len(handed),))],
        compiler_params=pltpu.CompilerParams(vmem_limit_bytes=VMEM_LIMIT),
        cost_estimate=pl.CostEstimate(flops=1 << 28, bytes_accessed=5 << 20, transcendentals=0),
    )(*between)
    return mixed, token_grad, gate_grad.T, grad_gate, grad_up, grad_down


def solution(mesh):
    rows = P(("dom", "blk", "sub", "rep"), None)
    weights = P("sub", "rep", "blk")
    grads = P(("dom", "sub"), "rep", "blk")
    return jax.shard_map(
        on_device,
        mesh=mesh,
        in_specs=(rows, rows, rows, weights, weights, weights, rows),
        out_specs=(rows, rows, rows, grads, grads, grads),
        check_vma=False,
    )
```

```python
import functools

import jax
import jax.numpy as jnp
from jax import lax
from jax.experimental import pallas as pl
from jax.experimental.pallas import tpu as pltpu
from jax.sharding import PartitionSpec as P

NUM_EXPERTS = 128
TOPK = 8
CAP = 12
VMEM_LIMIT = 60 << 20
MESH = pl.DeviceIdType.MESH
BF16 = jnp.bfloat16
F32 = jnp.float32


def each(low, high, body):
    if high - low <= 8:
        for i in range(low, high):
            body(i)
    else:

        def step(i, carry):
            body(i)
            return carry

        lax.fori_loop(low, high, step, 0)


def div_mod(k, n):
    if isinstance(k, int):
        return k // n, k % n
    return lax.div(k, n), lax.rem(k, n)


def steps_of(v, width, count):
    out = jnp.zeros_like(v)
    for m in range(1, count):
        out = out + (v >= m * width).astype(jnp.int32)
    return out


def dot(a, b):
    return jnp.dot(a, b, preferred_element_type=F32)


def dot_nt(a, b):
    return lax.dot_general(a, b, (((1,), (1,)), ((), ())), preferred_element_type=F32)


def dot_tn(a, b):
    return lax.dot_general(a, b, (((0,), (0,)), ((), ())), preferred_element_type=F32)


def as_mask(cond):
    return jnp.where(cond, 1.0, 0.0).astype(BF16)


def kernel(
    dims,
    ids_hbm,
    gw_hbm,
    tok_hbm,
    cot_hbm,
    wg_hbm,
    wu_hbm,
    wd_hbm,
    ids_ref,
    sel_ref,
    selw_ref,
    cots,
    xs,
    dos,
    hid,
    back,
    gw_ref,
    tok_ref,
    cot_ref,
    wg_ref,
    wu_ref,
    wd_ref,
    send1,
    recv1,
    part_own,
    part_send,
    part_from_left,
    part_from_right,
    px_own,
    px_send,
    px_recv,
    fin,
    in_s,
    disp_s,
    disp_r,
    fwd_s,
    fwd_r,
    rs_s,
    rs_left,
    rs_right,
    ag_s,
    ag_r,
    ag_l,
    px_s,
    px_r,
    bk_s,
    bk_r,
):
    n_blk, n_sub, n_rep, halves, pack = dims
    tok_count = tok_ref.shape[0]
    d_blk = wg_ref.shape[2]
    ff = wg_ref.shape[1]
    width = d_blk // halves
    per_blk = n_sub * n_rep
    chunk = per_blk * CAP
    rows = n_sub * pack
    kinds = 2 * halves
    pieces = hid.shape[1]
    unit = ff // pieces
    b = lax.axis_index("blk")
    s = lax.axis_index("sub")
    r = lax.axis_index("rep")
    other = 1 - r

    def wrap(v, n):
        return lax.rem(v + n, n)

    operands = (
        (ids_hbm, ids_ref),
        (gw_hbm, gw_ref),
        (tok_hbm, tok_ref),
        (cot_hbm, cot_ref),
        (wg_hbm, wg_ref),
        (wu_hbm, wu_ref),
        (wd_hbm, wd_ref),
    )
    fetches = [pltpu.make_async_copy(src, dst, in_s.at[i]) for i, (src, dst) in enumerate(operands)]
    for fetch in fetches:
        fetch.start()

    barrier = pltpu.get_barrier_semaphore()
    group = n_blk * n_sub * n_rep

    def greet(k):
        db, rest = div_mod(k, n_sub * n_rep)
        ds, dr = div_mod(rest, n_rep)
        pl.semaphore_signal(
            barrier,
            inc=1,
            device_id={"blk": wrap(b + db, n_blk), "sub": wrap(s + ds, n_sub), "rep": wrap(r + dr, n_rep)},
            device_id_type=MESH,
        )

    each(1, group, greet)

    for fetch in fetches[:2]:
        fetch.wait()

    sub_i = lax.broadcasted_iota(jnp.int32, (rows, tok_count), 0)
    sub_exp = steps_of(sub_i, pack, n_sub)
    sub_in = sub_i - sub_exp * pack
    sub_kind = steps_of(sub_in, CAP, kinds + 1)
    sub_slot = sub_in - sub_kind * CAP
    picked = jnp.zeros((rows, tok_count), F32)
    weight = jnp.zeros((rows, tok_count), F32)
    for k in range(ids_ref.shape[0]):
        hit = ids_ref[k : k + 1, :] == sub_exp
        picked = picked + jnp.where(hit, 1.0, 0.0)
        weight = weight + jnp.where(hit, gw_ref[k : k + 1, :], 0.0)
    row_i = lax.broadcasted_iota(jnp.int32, (tok_count, tok_count), 0)
    col_i = lax.broadcasted_iota(jnp.int32, (tok_count, tok_count), 1)
    before = dot(picked.astype(BF16), as_mask(row_i < col_i))
    placed = (before == sub_slot.astype(F32)) & (picked > 0.0) & (sub_kind < kinds)
    sel = jnp.where(placed, 1.0, 0.0)
    selw = jnp.where(placed, weight, 0.0)
    sel_ref[...] = sel
    selw_ref[...] = selw
    slot_gate = jnp.sum(selw, axis=1, keepdims=True)
    is_cot = sub_kind == 1
    for h in range(1, halves):
        is_cot = is_cot | (sub_kind == 2 * h + 1)
    row_scale = jnp.where(is_cot, jnp.broadcast_to(slot_gate, is_cot.shape), 1.0)[:, :1]
    takes = [jnp.where(sub_kind == x, sel, 0.0).astype(BF16) for x in range(kinds)]

    def columns(blk, h):
        return pl.ds(pl.multiple_of(blk * d_blk + h * width, width), width)

    my_q = b * per_blk + r * n_sub + s

    def disp_copy(k):
        db, ds = div_mod(k, n_sub)
        dst_b, dst_s = wrap(b + db, n_blk), wrap(s + ds, n_sub)
        return pltpu.make_async_remote_copy(
            src_ref=send1.at[dst_b, dst_s],
            dst_ref=recv1.at[my_q],
            send_sem=disp_s.at[k],
            recv_sem=disp_r.at[k],
            device_id={"blk": dst_b, "sub": dst_s},
            device_id_type=MESH,
        )

    def fwd_copy(k):
        db, ds = div_mod(k, n_sub)
        q = wrap(b - db, n_blk) * per_blk + r * n_sub + wrap(s - ds, n_sub)
        return pltpu.make_async_remote_copy(
            src_ref=recv1.at[q],
            dst_ref=recv1.at[q],
            send_sem=fwd_s.at[k],
            recv_sem=fwd_r.at[k],
            device_id={"rep": other},
            device_id_type=MESH,
        )

    def gather(db):
        blk = wrap(b + db, n_blk)
        acc = None
        for h in range(halves):
            cols = columns(blk, h)
            term = dot(takes[2 * h], tok_ref[:, cols]) + dot(takes[2 * h + 1], cot_ref[:, cols])
            acc = term if acc is None else acc + term
        send1[blk] = (acc * row_scale).astype(BF16).reshape(n_sub, pack, width)

    def send_rows(db):
        each(0, n_sub, lambda ds: disp_copy(db * n_sub + ds).start())

    for fetch in fetches[2:4]:
        fetch.wait()
    gather(1)
    pl.semaphore_wait(barrier, group - 1)
    send_rows(1)

    def gather_send(db):
        gather(db)
        send_rows(db)

    each(2, n_blk, gather_send)
    gather(0)
    each(1, n_sub, lambda ds: disp_copy(ds).start())
    recv1[my_q] = send1[b, s]
    fwd_copy(0).start()

    def forward(db):
        def one(ds):
            k = db * n_sub + ds
            disp_copy(k).wait_recv()
            fwd_copy(k).start()

        each(0, n_sub, one)

    def forward_first(ds):
        disp_copy(ds).wait_recv()
        fwd_copy(ds).start()

    each(1, n_sub, forward_first)

    prow = lax.broadcasted_iota(jnp.int32, (chunk, per_blk * pack), 0)
    pcol = lax.broadcasted_iota(jnp.int32, (chunk, per_blk * pack), 1)
    prow_g = steps_of(prow, CAP, per_blk)
    pcol_g = steps_of(pcol, pack, per_blk)
    prow_c = prow - prow_g * CAP
    pcol_j = pcol - pcol_g * pack
    unpack = [as_mask((prow_g == pcol_g) & (pcol_j == x * CAP + prow_c)) for x in range(kinds)]

    def cot_rows(db):
        blk = wrap(b + db, n_blk)
        acc = None
        for h in range(halves):
            term = dot(takes[2 * h], cot_ref[:, columns(blk, h)])
            acc = term if acc is None else acc + term
        cots[blk] = acc.astype(BF16)

    each(0, n_blk, cot_rows)

    def rs_copy(c, p, step):
        land, sems = (part_from_left, rs_left) if step == 1 else (part_from_right, rs_right)
        return pltpu.make_async_remote_copy(
            src_ref=part_send.at[c, p],
            dst_ref=land.at[c, p],
            send_sem=rs_s.at[c * pieces + p],
            recv_sem=sems.at[c * pieces + p],
            device_id={"blk": wrap(b + step, n_blk)},
            device_id_type=MESH,
        )

    def partial(db):
        blk = wrap(b - db, n_blk)
        each(0, n_sub, lambda ds: fwd_copy(db * n_sub + ds).wait_recv())
        block = recv1[pl.ds(blk * per_blk, per_blk)].reshape(per_blk * pack, width)
        for h in range(halves):
            xs[blk, :, h * width : (h + 1) * width] = dot(unpack[2 * h], block).astype(BF16)
            dos[blk, :, h * width : (h + 1) * width] = dot(unpack[2 * h + 1], block).astype(BF16)
        x, do = xs[blk], dos[blk]
        values = dot_nt(x, wg_ref[0]), dot_nt(x, wu_ref[0]), dot_nt(do, wd_ref[0])
        for m, value in enumerate(values):
            for p in range(pieces):
                part_own[blk, p, :, m * unit : (m + 1) * unit] = value[:, p * unit : (p + 1) * unit]

    for fetch in fetches[4:]:
        fetch.wait()
    forward(1)
    partial(0)

    def middle(db):
        forward(db + 1)
        partial(db)

    each(1, n_blk - 1, middle)
    partial(n_blk - 1)

    def push(c, p, step):
        land = part_from_left if step == 1 else part_from_right
        first = b == 0 if step == 1 else b == n_blk - 1

        @pl.when(first)
        def _():
            part_send[c, p] = part_own[c, p].astype(BF16)

        @pl.when(jnp.logical_not(first))
        def _():
            rs_copy(c, p, step).wait_recv()
            part_send[c, p] = (part_own[c, p] + land[c, p].astype(F32)).astype(BF16)

        rs_copy(c, p, step).start()

    def to_each(p, act):
        def one(k):
            @pl.when(n_blk - 1 - k > b)
            def _():
                act(n_blk - 1 - k, p, 1)

            @pl.when(k < b)
            def _():
                act(k, p, -1)

        each(0, n_blk - 1, one)

    def ag_copy(c, p, to, sem):
        return pltpu.make_async_remote_copy(
            src_ref=hid.at[c, p],
            dst_ref=hid.at[c, p],
            send_sem=sem,
            recv_sem=ag_r.at[c * pieces + p],
            device_id={"blk": to},
            device_id_type=MESH,
        )

    def to_right(p):
        return ag_copy(b, p, wrap(b + 1, n_blk), ag_s.at[b * pieces + p])

    def to_left(p):
        return ag_copy(b, p, wrap(b - 1, n_blk), ag_l.at[p])

    def both_ways(p, act):
        @pl.when(b + 1 < n_blk)
        def _():
            act(to_right(p))

        @pl.when(b >= 1)
        def _():
            act(to_left(p))

    def settle(p):
        @pl.when(b >= 1)
        def _():
            rs_copy(b, p, 1).wait_recv()
            part_own[b, p] += part_from_left[b, p].astype(F32)

        @pl.when(b + 1 < n_blk)
        def _():
            rs_copy(b, p, -1).wait_recv()
            part_own[b, p] += part_from_right[b, p].astype(F32)

        pre_gate = part_own[b, p, :, :unit]
        pre_up = part_own[b, p, :, unit : 2 * unit]
        dhid = part_own[b, p, :, 2 * unit :]
        sig = jax.nn.sigmoid(pre_gate)
        act = pre_gate * sig
        slope = sig * (1.0 + pre_gate * (1.0 - sig))
        hid[b, p, :, :unit] = (act * pre_up).astype(BF16)
        hid[b, p, :, unit : 2 * unit] = (dhid * pre_up * slope).astype(BF16)
        hid[b, p, :, 2 * unit :] = (dhid * act).astype(BF16)
        both_ways(p, lambda copy: copy.start())

    def pass_copy(c, p, step):
        return ag_copy(c, p, wrap(b + step, n_blk), ag_s.at[c * pieces + p])

    def take(c, p, step):
        pass_copy(c, p, step).wait_recv()

        @pl.when((b + step >= 0) & (b + step < n_blk))
        def _():
            pass_copy(c, p, step).start()

    def passed(c, step):
        for p in range(pieces):

            @pl.when((b + step >= 0) & (b + step < n_blk))
            def _():
                pass_copy(c, p, step).wait_send()

    def at_distance(d, fn):
        @pl.when(b - d >= 0)
        def _():
            fn(b - d, 1)

        @pl.when(b + d < n_blk)
        def _():
            fn(b + d, -1)

    def take_all(p):
        each(1, n_blk, lambda d: at_distance(d, lambda c, step: take(c, p, step)))

    to_each(0, push)
    for p in range(1, pieces):
        to_each(p, push)
        settle(p - 1)
        if p >= 2:
            take_all(p - 2)
    settle(pieces - 1)
    if pieces >= 2:
        take_all(pieces - 2)

    srow = lax.broadcasted_iota(jnp.int32, (rows, chunk), 0)
    scol = lax.broadcasted_iota(jnp.int32, (rows, chunk), 1)
    srow_s = steps_of(srow, pack, n_sub)
    srow_j = srow - srow_s * pack
    srow_x = steps_of(srow_j, CAP, kinds + 1)
    srow_at = srow_s * CAP + srow_j - srow_x * CAP

    def repack(rep):
        at = scol == srow_at + rep * (n_sub * CAP)
        return [as_mask(at & (srow_x == x)) for x in range(kinds)]

    to_mine, to_other = repack(r), repack(other)

    def px_copy(c):
        return pltpu.make_async_remote_copy(
            src_ref=px_send.at[c],
            dst_ref=px_recv.at[c],
            send_sem=px_s.at[c],
            recv_sem=px_r.at[c],
            device_id={"rep": other},
            device_id_type=MESH,
        )

    def bk_copy(c, dst_s):
        return pltpu.make_async_remote_copy(
            src_ref=fin.at[c, dst_s],
            dst_ref=back.at[b, s],
            send_sem=bk_s.at[c * n_sub + dst_s],
            recv_sem=bk_r.at[b * n_sub + s],
            device_id={"blk": c, "sub": dst_s},
            device_id_type=MESH,
        )

    def bk_arrival(k):
        db, ds = div_mod(k, n_sub)
        from_b, from_s = wrap(b + db, n_blk), wrap(s + ds, n_sub)
        return pltpu.make_async_remote_copy(
            src_ref=fin.at[from_b, from_s],
            dst_ref=back.at[from_b, from_s],
            send_sem=bk_s.at[from_b * n_sub + from_s],
            recv_sem=bk_r.at[from_b * n_sub + from_s],
            device_id={"blk": from_b, "sub": from_s},
            device_id_type=MESH,
        )

    def outputs(c, step):
        def whole(m):
            return jnp.concatenate([hid[c, p, :, m * unit : (m + 1) * unit] for p in range(pieces)], axis=1)

        out = dot(whole(0), wd_ref[0]).astype(BF16)
        into = (dot(whole(1), wg_ref[0]) + dot(whole(2), wu_ref[0])).astype(BF16)

        def packed(masks):
            acc = None
            for h in range(halves):
                cols = slice(h * width, (h + 1) * width)
                term = dot(masks[2 * h], out[:, cols]) + dot(masks[2 * h + 1], into[:, cols])
                acc = term if acc is None else acc + term
            return acc.astype(BF16).reshape(n_sub, pack, width)

        px_send[c] = packed(to_other)
        px_copy(c).start()
        px_own[c] = packed(to_mine)

    def finish(c, step):
        px_copy(c).wait_recv()
        fin[c] = (px_own[c].astype(F32) + px_recv[c].astype(F32)).astype(BF16)
        each(0, n_sub, lambda dst_s: bk_copy(c, dst_s).start())

    outputs(b, 0)

    def rest(d):
        at_distance(d, lambda c, step: take(c, pieces - 1, step))
        at_distance(d, outputs)
        at_distance(d, finish)

    each(1, n_blk, rest)
    px_copy(b).wait_recv()
    fin[b] = (px_own[b].astype(F32) + px_recv[b].astype(F32)).astype(BF16)
    each(1, n_sub, lambda ds: bk_copy(b, wrap(s + ds, n_sub)).start())
    back[b, s] = fin[b, s]
    each(1, n_blk * n_sub, lambda k: bk_arrival(k).wait_recv())

    each(1, n_blk * n_sub, lambda k: disp_copy(k).wait_send())
    each(0, n_blk * n_sub, lambda k: fwd_copy(k).wait_send())
    for p in range(pieces):
        to_each(p, lambda c, p, step: rs_copy(c, p, step).wait_send())
        both_ways(p, lambda copy: copy.wait_send())
    each(1, n_blk, lambda d: at_distance(d, passed))
    each(0, n_blk, lambda c: px_copy(c).wait_send())
    each(1, n_blk * n_sub, lambda k: bk_arrival(k).wait_send())


def finish_kernel(
    dims,
    ids_hbm,
    sel_hbm,
    selw_hbm,
    cots_hbm,
    xs_hbm,
    dos_hbm,
    hid_hbm,
    back_hbm,
    mixed_hbm,
    tgrad_hbm,
    ggrad_hbm,
    gg_hbm,
    gu_hbm,
    gd_hbm,
    mixed_ref,
    tgrad_ref,
    ggrad_ref,
    gg_ref,
    gu_ref,
    gd_ref,
    ids_ref,
    sel_ref,
    selw_ref,
    cots,
    xs,
    dos,
    hid,
    back,
    sems,
    in_sems,
):
    n_blk, n_sub, halves, pack, scale = dims
    d_blk = xs.shape[2]
    all_rows = n_blk * xs.shape[1]
    pieces, unit = hid.shape[1], hid.shape[3] // 3
    width = d_blk // halves
    rows = n_sub * pack
    kinds = 2 * halves
    pairs = (
        (mixed_ref, mixed_hbm),
        (tgrad_ref, tgrad_hbm),
        (ggrad_ref, ggrad_hbm),
        (gg_ref, gg_hbm),
        (gu_ref, gu_hbm),
        (gd_ref, gd_hbm),
    )
    outs = [pltpu.make_async_copy(src, dst, sems.at[i]) for i, (src, dst) in enumerate(pairs)]
    operands = (
        (xs_hbm, xs),
        (hid_hbm, hid),
        (dos_hbm, dos),
        (ids_hbm, ids_ref),
        (sel_hbm, sel_ref),
        (selw_hbm, selw_ref),
        (cots_hbm, cots),
        (back_hbm, back),
    )
    fetches = [pltpu.make_async_copy(src, dst, in_sems.at[i]) for i, (src, dst) in enumerate(operands)]
    for fetch in fetches:
        fetch.start()
    for fetch in fetches[:3]:
        fetch.wait()
    x_all = xs[...].reshape(all_rows, d_blk)
    do_all = dos[...].reshape(all_rows, d_blk)

    def weight_grad(m, right, out_ref):
        for p in range(pieces):
            left = hid[:, p, :, m * unit : (m + 1) * unit].reshape(all_rows, unit)
            out_ref[0, p * unit : (p + 1) * unit, :] = dot_tn(left, right) * scale

    weight_grad(1, x_all, gg_ref)
    outs[3].start()
    weight_grad(2, x_all, gu_ref)
    outs[4].start()
    weight_grad(0, do_all, gd_ref)
    outs[5].start()

    for fetch in fetches[3:]:
        fetch.wait()
    tok_count = sel_ref.shape[1]
    sub_i = lax.broadcasted_iota(jnp.int32, (rows, tok_count), 0)
    sub_exp = steps_of(sub_i, pack, n_sub)
    sub_kind = steps_of(sub_i - sub_exp * pack, CAP, kinds + 1)
    selw = selw_ref[...]
    high = selw.astype(BF16).astype(F32)
    low = selw - high
    takes = []
    for h in range(halves):
        mine = sub_kind == 2 * h
        takes.append(
            [
                jnp.where(mine, high, 0.0).T.astype(BF16),
                jnp.where(mine, low, 0.0).T.astype(BF16),
                jnp.where(sub_kind == 2 * h + 1, sel_ref[...], 0.0).T.astype(BF16),
            ]
        )
    dots = jnp.zeros((rows, 1), F32)
    for blk in range(n_blk):
        got = back[blk].reshape(rows, width)
        for h in range(halves):
            cols = slice(blk * d_blk + h * width, blk * d_blk + (h + 1) * width)
            high_t, low_t, ones_t = takes[h]
            mixed_ref[:, cols] = (dot(high_t, got) + dot(low_t, got)).astype(BF16)
            tgrad_ref[:, cols] = dot(ones_t, got).astype(BF16)
        dots = dots + jnp.sum(cots[blk].astype(F32) * got.astype(F32), axis=1, keepdims=True)
    outs[0].start()
    outs[1].start()
    token_dots = sel_ref[...] * dots
    for k in range(ids_ref.shape[0]):
        hit = ids_ref[k : k + 1, :] == sub_exp
        ggrad_ref[k : k + 1, :] = jnp.sum(jnp.where(hit, token_dots, 0.0), axis=0, keepdims=True)
    outs[2].start()
    for out in outs:
        out.wait()


def on_device(tokens, expert_ids, gate_weights, w_gate, w_up, w_down, cotangent):
    n_blk, n_sub, n_rep = (lax.axis_size(name) for name in ("blk", "sub", "rep"))
    tok_count, d_model = tokens.shape
    _, ff, d_blk = w_gate.shape
    scale = (tok_count * n_blk * n_sub * n_rep * TOPK / NUM_EXPERTS) ** (-0.5)
    halves = 2 if d_blk % 256 == 0 else 1
    width = d_blk // halves
    pack = -(-2 * halves * CAP // 16) * 16
    rows = n_sub * pack
    chunk = n_sub * n_rep * CAP
    pairs = n_blk * n_sub
    dma = pltpu.SemaphoreType.DMA
    vmem = pl.BlockSpec(memory_space=pltpu.VMEM)
    anywhere = pl.BlockSpec(memory_space=pl.ANY)
    packed = (n_blk, n_sub, pack, width)
    shaped = jax.ShapeDtypeStruct
    pieces = ff // 128 if ff % 128 == 0 else 1
    spread = (n_blk, pieces, chunk, 3 * ff // pieces)
    ids, gates = expert_ids.T, gate_weights.T
    handed = (
        shaped(ids.shape, ids.dtype),
        shaped((rows, tok_count), F32),
        shaped((rows, tok_count), F32),
        shaped((n_blk, rows, width), BF16),
        shaped((n_blk, chunk, d_blk), BF16),
        shaped((n_blk, chunk, d_blk), BF16),
        shaped(spread, BF16),
        shaped(packed, BF16),
    )
    held = [
        (gates.shape, F32),
        (tokens.shape, BF16),
        (tokens.shape, BF16),
        ((1, ff, d_blk), BF16),
        ((1, ff, d_blk), BF16),
        ((1, ff, d_blk), BF16),
        (packed, BF16),
        ((pairs * n_rep, pack, width), BF16),
        (spread, F32),
        (spread, BF16),
        (spread, BF16),
        (spread, BF16),
        (packed, BF16),
        (packed, BF16),
        (packed, BF16),
        (packed, BF16),
    ]
    between = pl.pallas_call(
        functools.partial(kernel, (n_blk, n_sub, n_rep, halves, pack)),
        out_shape=handed,
        in_specs=[pl.BlockSpec(memory_space=pltpu.HBM)] * 7,
        out_specs=(vmem,) * len(handed),
        scratch_shapes=[pltpu.VMEM(shape, kind) for shape, kind in held]
        + [dma((7,))]
        + [dma((pairs,))] * 4
        + [dma((n_blk * pieces,))] * 5
        + [dma((pieces,))]
        + [dma((n_blk,))] * 2
        + [dma((pairs,))] * 2,
        compiler_params=pltpu.CompilerParams(
            collective_id=0,
            has_side_effects=True,
            vmem_limit_bytes=VMEM_LIMIT,
        ),
        cost_estimate=pl.CostEstimate(flops=1 << 30, bytes_accessed=8 << 20, transcendentals=chunk * ff),
    )(ids, gates, tokens, cotangent, w_gate, w_up, w_down)
    grad = shaped((1, ff, d_blk), F32)
    results = (
        shaped((tok_count, d_model), BF16),
        shaped((tok_count, d_model), BF16),
        shaped(gates.shape, F32),
        grad,
        grad,
        grad,
    )
    mixed, token_grad, gate_grad, grad_gate, grad_up, grad_down = pl.pallas_call(
        functools.partial(finish_kernel, (n_blk, n_sub, halves, pack, scale)),
        out_shape=results,
        in_specs=[anywhere] * len(handed),
        out_specs=(anywhere,) * len(results),
        scratch_shapes=[pltpu.VMEM(one.shape, one.dtype) for one in results + handed]
        + [dma((len(results),)), dma((len(handed),))],
        compiler_params=pltpu.CompilerParams(vmem_limit_bytes=VMEM_LIMIT),
        cost_estimate=pl.CostEstimate(flops=1 << 28, bytes_accessed=5 << 20, transcendentals=0),
    )(*between)
    return mixed, token_grad, gate_grad.T, grad_gate, grad_up, grad_down


def solution(mesh):
    rows = P(("dom", "blk", "sub", "rep"), None)
    weights = P("sub", "rep", "blk")
    grads = P(("dom", "sub"), "rep", "blk")
    return jax.shard_map(
        on_device,
        mesh=mesh,
        in_specs=(rows, rows, rows, weights, weights, weights, rows),
        out_specs=(rows, rows, rows, grads, grads, grads),
        check_vma=False,
    )
```

```python
import functools

import jax
import jax.numpy as jnp
from jax import lax
from jax.experimental import pallas as pl
from jax.experimental.pallas import tpu as pltpu
from jax.sharding import PartitionSpec as P

NUM_EXPERTS = 128
TOPK = 8
CAP = 12
VMEM_LIMIT = 60 << 20
MESH = pl.DeviceIdType.MESH
BF16 = jnp.bfloat16
F32 = jnp.float32


def each(low, high, body):
    if high - low <= 8:
        for i in range(low, high):
            body(i)
    else:

        def step(i, carry):
            body(i)
            return carry

        lax.fori_loop(low, high, step, 0)


def div_mod(k, n):
    if isinstance(k, int):
        return k // n, k % n
    return lax.div(k, n), lax.rem(k, n)


def steps_of(v, width, count):
    out = jnp.zeros_like(v)
    for m in range(1, count):
        out = out + (v >= m * width).astype(jnp.int32)
    return out


def dot(a, b):
    return jnp.dot(a, b, preferred_element_type=F32)


def dot_nt(a, b):
    return lax.dot_general(a, b, (((1,), (1,)), ((), ())), preferred_element_type=F32)


def dot_tn(a, b):
    return lax.dot_general(a, b, (((0,), (0,)), ((), ())), preferred_element_type=F32)


def as_mask(cond):
    return jnp.where(cond, 1.0, 0.0).astype(BF16)


def kernel(
    dims,
    ids_hbm,
    gw_hbm,
    tok_hbm,
    cot_hbm,
    wg_hbm,
    wu_hbm,
    wd_hbm,
    ids_ref,
    sel_ref,
    selw_ref,
    cots,
    xs,
    dos,
    hid,
    back,
    gw_ref,
    tok_ref,
    cot_ref,
    wg_ref,
    wu_ref,
    wd_ref,
    send1,
    recv1,
    part_own,
    part_send,
    part_recv,
    px_own,
    px_send,
    px_recv,
    fin,
    in_s,
    disp_s,
    disp_r,
    fwd_s,
    fwd_r,
    rs_s,
    rs_r,
    ag_s,
    ag_r,
    ag_l,
    ag_far,
    px_s,
    px_r,
    bk_s,
    bk_r,
):
    n_blk, n_sub, n_rep, halves, pack = dims
    tok_count = tok_ref.shape[0]
    d_blk = wg_ref.shape[2]
    ff = wg_ref.shape[1]
    width = d_blk // halves
    per_blk = n_sub * n_rep
    chunk = per_blk * CAP
    rows = n_sub * pack
    kinds = 2 * halves
    pieces = hid.shape[1]
    unit = ff // pieces
    b = lax.axis_index("blk")
    s = lax.axis_index("sub")
    r = lax.axis_index("rep")
    other = 1 - r

    def wrap(v, n):
        return lax.rem(v + n, n)

    operands = (
        (ids_hbm, ids_ref),
        (gw_hbm, gw_ref),
        (tok_hbm, tok_ref),
        (cot_hbm, cot_ref),
        (wg_hbm, wg_ref),
        (wu_hbm, wu_ref),
        (wd_hbm, wd_ref),
    )
    fetches = [pltpu.make_async_copy(src, dst, in_s.at[i]) for i, (src, dst) in enumerate(operands)]
    for fetch in fetches:
        fetch.start()

    barrier = pltpu.get_barrier_semaphore()
    group = n_blk * n_sub * n_rep

    def greet(k):
        db, rest = div_mod(k, n_sub * n_rep)
        ds, dr = div_mod(rest, n_rep)
        pl.semaphore_signal(
            barrier,
            inc=1,
            device_id={"blk": wrap(b + db, n_blk), "sub": wrap(s + ds, n_sub), "rep": wrap(r + dr, n_rep)},
            device_id_type=MESH,
        )

    each(1, group, greet)

    for fetch in fetches[:2]:
        fetch.wait()

    sub_i = lax.broadcasted_iota(jnp.int32, (rows, tok_count), 0)
    sub_exp = steps_of(sub_i, pack, n_sub)
    sub_in = sub_i - sub_exp * pack
    sub_kind = steps_of(sub_in, CAP, kinds + 1)
    sub_slot = sub_in - sub_kind * CAP
    picked = jnp.zeros((rows, tok_count), F32)
    weight = jnp.zeros((rows, tok_count), F32)
    for k in range(ids_ref.shape[0]):
        hit = ids_ref[k : k + 1, :] == sub_exp
        picked = picked + jnp.where(hit, 1.0, 0.0)
        weight = weight + jnp.where(hit, gw_ref[k : k + 1, :], 0.0)
    row_i = lax.broadcasted_iota(jnp.int32, (tok_count, tok_count), 0)
    col_i = lax.broadcasted_iota(jnp.int32, (tok_count, tok_count), 1)
    before = dot(picked.astype(BF16), as_mask(row_i < col_i))
    placed = (before == sub_slot.astype(F32)) & (picked > 0.0) & (sub_kind < kinds)
    sel = jnp.where(placed, 1.0, 0.0)
    selw = jnp.where(placed, weight, 0.0)
    sel_ref[...] = sel
    selw_ref[...] = selw
    slot_gate = jnp.sum(selw, axis=1, keepdims=True)
    is_cot = sub_kind == 1
    for h in range(1, halves):
        is_cot = is_cot | (sub_kind == 2 * h + 1)
    row_scale = jnp.where(is_cot, jnp.broadcast_to(slot_gate, is_cot.shape), 1.0)[:, :1]
    takes = [jnp.where(sub_kind == x, sel, 0.0).astype(BF16) for x in range(kinds)]

    def columns(blk, h):
        return pl.ds(pl.multiple_of(blk * d_blk + h * width, width), width)

    my_q = b * per_blk + r * n_sub + s

    def disp_copy(k):
        db, ds = div_mod(k, n_sub)
        dst_b, dst_s = wrap(b + db, n_blk), wrap(s + ds, n_sub)
        return pltpu.make_async_remote_copy(
            src_ref=send1.at[dst_b, dst_s],
            dst_ref=recv1.at[my_q],
            send_sem=disp_s.at[k],
            recv_sem=disp_r.at[k],
            device_id={"blk": dst_b, "sub": dst_s},
            device_id_type=MESH,
        )

    def fwd_copy(k):
        db, ds = div_mod(k, n_sub)
        q = wrap(b - db, n_blk) * per_blk + r * n_sub + wrap(s - ds, n_sub)
        return pltpu.make_async_remote_copy(
            src_ref=recv1.at[q],
            dst_ref=recv1.at[q],
            send_sem=fwd_s.at[k],
            recv_sem=fwd_r.at[k],
            device_id={"rep": other},
            device_id_type=MESH,
        )

    def gather(db):
        blk = wrap(b + db, n_blk)
        acc = None
        for h in range(halves):
            cols = columns(blk, h)
            term = dot(takes[2 * h], tok_ref[:, cols]) + dot(takes[2 * h + 1], cot_ref[:, cols])
            acc = term if acc is None else acc + term
        send1[blk] = (acc * row_scale).astype(BF16).reshape(n_sub, pack, width)

    def send_rows(db):
        each(0, n_sub, lambda ds: disp_copy(db * n_sub + ds).start())

    for fetch in fetches[2:4]:
        fetch.wait()
    gather(1)
    pl.semaphore_wait(barrier, group - 1)
    send_rows(1)

    def gather_send(db):
        gather(db)
        send_rows(db)

    each(2, n_blk, gather_send)
    gather(0)
    each(1, n_sub, lambda ds: disp_copy(ds).start())
    recv1[my_q] = send1[b, s]
    fwd_copy(0).start()

    def forward(db):
        def one(ds):
            k = db * n_sub + ds
            disp_copy(k).wait_recv()
            fwd_copy(k).start()

        each(0, n_sub, one)

    def forward_first(ds):
        disp_copy(ds).wait_recv()
        fwd_copy(ds).start()

    each(1, n_sub, forward_first)

    prow = lax.broadcasted_iota(jnp.int32, (chunk, per_blk * pack), 0)
    pcol = lax.broadcasted_iota(jnp.int32, (chunk, per_blk * pack), 1)
    prow_g = steps_of(prow, CAP, per_blk)
    pcol_g = steps_of(pcol, pack, per_blk)
    prow_c = prow - prow_g * CAP
    pcol_j = pcol - pcol_g * pack
    unpack = [as_mask((prow_g == pcol_g) & (pcol_j == x * CAP + prow_c)) for x in range(kinds)]

    def cot_rows(db):
        blk = wrap(b + db, n_blk)
        acc = None
        for h in range(halves):
            term = dot(takes[2 * h], cot_ref[:, columns(blk, h)])
            acc = term if acc is None else acc + term
        cots[blk] = acc.astype(BF16)

    each(0, n_blk, cot_rows)

    def rs_copy(db, p):
        return pltpu.make_async_remote_copy(
            src_ref=part_send.at[db, p],
            dst_ref=part_recv.at[db, p],
            send_sem=rs_s.at[db * pieces + p],
            recv_sem=rs_r.at[db * pieces + p],
            device_id={"blk": wrap(b - db, n_blk)},
            device_id_type=MESH,
        )

    def partial(db):
        blk = wrap(b - db, n_blk)
        each(0, n_sub, lambda ds: fwd_copy(db * n_sub + ds).wait_recv())
        block = recv1[pl.ds(blk * per_blk, per_blk)].reshape(per_blk * pack, width)
        for h in range(halves):
            xs[blk, :, h * width : (h + 1) * width] = dot(unpack[2 * h], block).astype(BF16)
            dos[blk, :, h * width : (h + 1) * width] = dot(unpack[2 * h + 1], block).astype(BF16)
        x, do = xs[blk], dos[blk]
        return dot_nt(x, wg_ref[0]), dot_nt(x, wu_ref[0]), dot_nt(do, wd_ref[0])

    def partial_send(db):
        values = partial(db)
        for p in range(pieces):
            for m, value in enumerate(values):
                part_send[db, p, :, m * unit : (m + 1) * unit] = value[:, p * unit : (p + 1) * unit].astype(BF16)
            rs_copy(db, p).start()

    for fetch in fetches[4:]:
        fetch.wait()
    forward(1)
    for m, value in enumerate(partial(0)):
        for p in range(pieces):
            part_own[p, :, m * unit : (m + 1) * unit] = value[:, p * unit : (p + 1) * unit]

    def middle(db):
        forward(db + 1)
        partial_send(db)

    each(1, n_blk - 1, middle)
    partial_send(n_blk - 1)

    def ag_copy(c, p, to, sem):
        return pltpu.make_async_remote_copy(
            src_ref=hid.at[c, p],
            dst_ref=hid.at[c, p],
            send_sem=sem,
            recv_sem=ag_r.at[c * pieces + p],
            device_id={"blk": to},
            device_id_type=MESH,
        )

    def to_right(p):
        return ag_copy(b, p, wrap(b + 1, n_blk), ag_s.at[b * pieces + p])

    def to_left(p):
        return ag_copy(b, p, wrap(b - 1, n_blk), ag_l.at[p])

    def both_ways(p, act):
        @pl.when(b + 2 < n_blk)
        def _():
            act(ag_copy(b, p, wrap(b + 2, n_blk), ag_far.at[p, 0]))

        @pl.when(b >= 2)
        def _():
            act(ag_copy(b, p, wrap(b - 2, n_blk), ag_far.at[p, 1]))

        @pl.when(b + 1 < n_blk)
        def _():
            act(to_right(p))

        @pl.when(b >= 1)
        def _():
            act(to_left(p))

    for p in range(pieces):

        def add_part(db):
            rs_copy(db, p).wait_recv()
            part_own[p] += part_recv[db, p].astype(F32)

        each(1, n_blk, add_part)
        pre_gate = part_own[p, :, :unit]
        pre_up = part_own[p, :, unit : 2 * unit]
        dhid = part_own[p, :, 2 * unit :]
        sig = jax.nn.sigmoid(pre_gate)
        act = pre_gate * sig
        slope = sig * (1.0 + pre_gate * (1.0 - sig))
        hid[b, p, :, :unit] = (act * pre_up).astype(BF16)
        hid[b, p, :, unit : 2 * unit] = (dhid * pre_up * slope).astype(BF16)
        hid[b, p, :, 2 * unit :] = (dhid * act).astype(BF16)
        both_ways(p, lambda copy: copy.start())

    def pass_copy(c, p, step):
        return ag_copy(c, p, wrap(b + step, n_blk), ag_s.at[c * pieces + p])

    def onward(d, step):
        return (d >= 2) & (b + step >= 0) & (b + step < n_blk)

    def take(d):
        def one(c, step):
            for p in range(pieces):
                pass_copy(c, p, step).wait_recv()

                @pl.when(onward(d, step))
                def _():
                    pass_copy(c, p, step).start()

        at_distance(d, one)

    def passed(d):
        def one(c, step):
            for p in range(pieces):

                @pl.when(onward(d, step))
                def _():
                    pass_copy(c, p, step).wait_send()

        at_distance(d, one)

    def at_distance(d, fn):
        @pl.when(b - d >= 0)
        def _():
            fn(b - d, 1)

        @pl.when(b + d < n_blk)
        def _():
            fn(b + d, -1)

    srow = lax.broadcasted_iota(jnp.int32, (rows, chunk), 0)
    scol = lax.broadcasted_iota(jnp.int32, (rows, chunk), 1)
    srow_s = steps_of(srow, pack, n_sub)
    srow_j = srow - srow_s * pack
    srow_x = steps_of(srow_j, CAP, kinds + 1)
    srow_at = srow_s * CAP + srow_j - srow_x * CAP

    def repack(rep):
        at = scol == srow_at + rep * (n_sub * CAP)
        return [as_mask(at & (srow_x == x)) for x in range(kinds)]

    to_mine, to_other = repack(r), repack(other)

    def px_copy(c):
        return pltpu.make_async_remote_copy(
            src_ref=px_send.at[c],
            dst_ref=px_recv.at[c],
            send_sem=px_s.at[c],
            recv_sem=px_r.at[c],
            device_id={"rep": other},
            device_id_type=MESH,
        )

    def bk_copy(c, dst_s):
        return pltpu.make_async_remote_copy(
            src_ref=fin.at[c, dst_s],
            dst_ref=back.at[b, s],
            send_sem=bk_s.at[c * n_sub + dst_s],
            recv_sem=bk_r.at[b * n_sub + s],
            device_id={"blk": c, "sub": dst_s},
            device_id_type=MESH,
        )

    def bk_arrival(k):
        db, ds = div_mod(k, n_sub)
        from_b, from_s = wrap(b + db, n_blk), wrap(s + ds, n_sub)
        return pltpu.make_async_remote_copy(
            src_ref=fin.at[from_b, from_s],
            dst_ref=back.at[from_b, from_s],
            send_sem=bk_s.at[from_b * n_sub + from_s],
            recv_sem=bk_r.at[from_b * n_sub + from_s],
            device_id={"blk": from_b, "sub": from_s},
            device_id_type=MESH,
        )

    def outputs(c, step):
        def whole(m):
            return jnp.concatenate([hid[c, p, :, m * unit : (m + 1) * unit] for p in range(pieces)], axis=1)

        out = dot(whole(0), wd_ref[0]).astype(BF16)
        into = (dot(whole(1), wg_ref[0]) + dot(whole(2), wu_ref[0])).astype(BF16)

        def packed(masks):
            acc = None
            for h in range(halves):
                cols = slice(h * width, (h + 1) * width)
                term = dot(masks[2 * h], out[:, cols]) + dot(masks[2 * h + 1], into[:, cols])
                acc = term if acc is None else acc + term
            return acc.astype(BF16).reshape(n_sub, pack, width)

        px_send[c] = packed(to_other)
        px_copy(c).start()
        px_own[c] = packed(to_mine)

    def finish(c, step):
        px_copy(c).wait_recv()
        fin[c] = (px_own[c].astype(F32) + px_recv[c].astype(F32)).astype(BF16)
        each(0, n_sub, lambda dst_s: bk_copy(c, dst_s).start())

    outputs(b, 0)

    def near(d):
        take(d)
        take(d + 1)
        at_distance(d, outputs)
        at_distance(d + 1, outputs)
        at_distance(d, finish)
        at_distance(d + 1, finish)

    each(0, (n_blk - 1) // 2, lambda i: near(1 + 2 * i))
    if n_blk % 2 == 0:
        take(n_blk - 1)
        at_distance(n_blk - 1, outputs)
        at_distance(n_blk - 1, finish)
    px_copy(b).wait_recv()
    fin[b] = (px_own[b].astype(F32) + px_recv[b].astype(F32)).astype(BF16)
    each(1, n_sub, lambda ds: bk_copy(b, wrap(s + ds, n_sub)).start())
    back[b, s] = fin[b, s]
    each(1, n_blk * n_sub, lambda k: bk_arrival(k).wait_recv())

    each(1, n_blk * n_sub, lambda k: disp_copy(k).wait_send())
    each(0, n_blk * n_sub, lambda k: fwd_copy(k).wait_send())
    for p in range(pieces):
        each(1, n_blk, lambda db: rs_copy(db, p).wait_send())
        both_ways(p, lambda copy: copy.wait_send())
    each(2, n_blk, passed)
    each(0, n_blk, lambda c: px_copy(c).wait_send())
    each(1, n_blk * n_sub, lambda k: bk_arrival(k).wait_send())


def finish_kernel(
    dims,
    ids_hbm,
    sel_hbm,
    selw_hbm,
    cots_hbm,
    xs_hbm,
    dos_hbm,
    hid_hbm,
    back_hbm,
    mixed_hbm,
    tgrad_hbm,
    ggrad_hbm,
    gg_hbm,
    gu_hbm,
    gd_hbm,
    mixed_ref,
    tgrad_ref,
    ggrad_ref,
    gg_ref,
    gu_ref,
    gd_ref,
    ids_ref,
    sel_ref,
    selw_ref,
    cots,
    xs,
    dos,
    hid,
    back,
    sems,
    in_sems,
):
    n_blk, n_sub, halves, pack, scale = dims
    d_blk = xs.shape[2]
    all_rows = n_blk * xs.shape[1]
    pieces, unit = hid.shape[1], hid.shape[3] // 3
    width = d_blk // halves
    rows = n_sub * pack
    kinds = 2 * halves
    pairs = (
        (mixed_ref, mixed_hbm),
        (tgrad_ref, tgrad_hbm),
        (ggrad_ref, ggrad_hbm),
        (gg_ref, gg_hbm),
        (gu_ref, gu_hbm),
        (gd_ref, gd_hbm),
    )
    outs = [pltpu.make_async_copy(src, dst, sems.at[i]) for i, (src, dst) in enumerate(pairs)]
    operands = (
        (xs_hbm, xs),
        (hid_hbm, hid),
        (dos_hbm, dos),
        (ids_hbm, ids_ref),
        (sel_hbm, sel_ref),
        (selw_hbm, selw_ref),
        (cots_hbm, cots),
        (back_hbm, back),
    )
    fetches = [pltpu.make_async_copy(src, dst, in_sems.at[i]) for i, (src, dst) in enumerate(operands)]
    for fetch in fetches:
        fetch.start()
    for fetch in fetches[:3]:
        fetch.wait()
    x_all = xs[...].reshape(all_rows, d_blk)
    do_all = dos[...].reshape(all_rows, d_blk)

    def weight_grad(m, right, out_ref):
        for p in range(pieces):
            left = hid[:, p, :, m * unit : (m + 1) * unit].reshape(all_rows, unit)
            out_ref[0, p * unit : (p + 1) * unit, :] = dot_tn(left, right) * scale

    weight_grad(1, x_all, gg_ref)
    outs[3].start()
    weight_grad(2, x_all, gu_ref)
    outs[4].start()
    weight_grad(0, do_all, gd_ref)
    outs[5].start()

    for fetch in fetches[3:]:
        fetch.wait()
    tok_count = sel_ref.shape[1]
    sub_i = lax.broadcasted_iota(jnp.int32, (rows, tok_count), 0)
    sub_exp = steps_of(sub_i, pack, n_sub)
    sub_kind = steps_of(sub_i - sub_exp * pack, CAP, kinds + 1)
    selw = selw_ref[...]
    high = selw.astype(BF16).astype(F32)
    low = selw - high
    takes = []
    for h in range(halves):
        mine = sub_kind == 2 * h
        takes.append(
            [
                jnp.where(mine, high, 0.0).T.astype(BF16),
                jnp.where(mine, low, 0.0).T.astype(BF16),
                jnp.where(sub_kind == 2 * h + 1, sel_ref[...], 0.0).T.astype(BF16),
            ]
        )
    dots = jnp.zeros((rows, 1), F32)
    for blk in range(n_blk):
        got = back[blk].reshape(rows, width)
        for h in range(halves):
            cols = slice(blk * d_blk + h * width, blk * d_blk + (h + 1) * width)
            high_t, low_t, ones_t = takes[h]
            mixed_ref[:, cols] = (dot(high_t, got) + dot(low_t, got)).astype(BF16)
            tgrad_ref[:, cols] = dot(ones_t, got).astype(BF16)
        dots = dots + jnp.sum(cots[blk].astype(F32) * got.astype(F32), axis=1, keepdims=True)
    outs[0].start()
    outs[1].start()
    token_dots = sel_ref[...] * dots
    for k in range(ids_ref.shape[0]):
        hit = ids_ref[k : k + 1, :] == sub_exp
        ggrad_ref[k : k + 1, :] = jnp.sum(jnp.where(hit, token_dots, 0.0), axis=0, keepdims=True)
    outs[2].start()
    for out in outs:
        out.wait()


def on_device(tokens, expert_ids, gate_weights, w_gate, w_up, w_down, cotangent):
    n_blk, n_sub, n_rep = (lax.axis_size(name) for name in ("blk", "sub", "rep"))
    tok_count, d_model = tokens.shape
    _, ff, d_blk = w_gate.shape
    scale = (tok_count * n_blk * n_sub * n_rep * TOPK / NUM_EXPERTS) ** (-0.5)
    halves = 2 if d_blk % 256 == 0 else 1
    width = d_blk // halves
    pack = -(-2 * halves * CAP // 16) * 16
    rows = n_sub * pack
    chunk = n_sub * n_rep * CAP
    pairs = n_blk * n_sub
    dma = pltpu.SemaphoreType.DMA
    vmem = pl.BlockSpec(memory_space=pltpu.VMEM)
    anywhere = pl.BlockSpec(memory_space=pl.ANY)
    packed = (n_blk, n_sub, pack, width)
    shaped = jax.ShapeDtypeStruct
    pieces = ff // 128 if ff % 128 == 0 else 1
    spread = (n_blk, pieces, chunk, 3 * ff // pieces)
    ids, gates = expert_ids.T, gate_weights.T
    handed = (
        shaped(ids.shape, ids.dtype),
        shaped((rows, tok_count), F32),
        shaped((rows, tok_count), F32),
        shaped((n_blk, rows, width), BF16),
        shaped((n_blk, chunk, d_blk), BF16),
        shaped((n_blk, chunk, d_blk), BF16),
        shaped(spread, BF16),
        shaped(packed, BF16),
    )
    held = [
        (gates.shape, F32),
        (tokens.shape, BF16),
        (tokens.shape, BF16),
        ((1, ff, d_blk), BF16),
        ((1, ff, d_blk), BF16),
        ((1, ff, d_blk), BF16),
        (packed, BF16),
        ((pairs * n_rep, pack, width), BF16),
        (spread[1:], F32),
        (spread, BF16),
        (spread, BF16),
        (packed, BF16),
        (packed, BF16),
        (packed, BF16),
        (packed, BF16),
    ]
    between = pl.pallas_call(
        functools.partial(kernel, (n_blk, n_sub, n_rep, halves, pack)),
        out_shape=handed,
        in_specs=[pl.BlockSpec(memory_space=pltpu.HBM)] * 7,
        out_specs=(vmem,) * len(handed),
        scratch_shapes=[pltpu.VMEM(shape, kind) for shape, kind in held]
        + [dma((7,))]
        + [dma((pairs,))] * 4
        + [dma((n_blk * pieces,))] * 4
        + [dma((pieces,)), dma((pieces, 2))]
        + [dma((n_blk,))] * 2
        + [dma((pairs,))] * 2,
        compiler_params=pltpu.CompilerParams(
            collective_id=0,
            has_side_effects=True,
            vmem_limit_bytes=VMEM_LIMIT,
        ),
        cost_estimate=pl.CostEstimate(flops=1 << 30, bytes_accessed=8 << 20, transcendentals=chunk * ff),
    )(ids, gates, tokens, cotangent, w_gate, w_up, w_down)
    grad = shaped((1, ff, d_blk), F32)
    results = (
        shaped((tok_count, d_model), BF16),
        shaped((tok_count, d_model), BF16),
        shaped(gates.shape, F32),
        grad,
        grad,
        grad,
    )
    mixed, token_grad, gate_grad, grad_gate, grad_up, grad_down = pl.pallas_call(
        functools.partial(finish_kernel, (n_blk, n_sub, halves, pack, scale)),
        out_shape=results,
        in_specs=[anywhere] * len(handed),
        out_specs=(anywhere,) * len(results),
        scratch_shapes=[pltpu.VMEM(one.shape, one.dtype) for one in results + handed]
        + [dma((len(results),)), dma((len(handed),))],
        compiler_params=pltpu.CompilerParams(vmem_limit_bytes=VMEM_LIMIT),
        cost_estimate=pl.CostEstimate(flops=1 << 28, bytes_accessed=5 << 20, transcendentals=0),
    )(*between)
    return mixed, token_grad, gate_grad.T, grad_gate, grad_up, grad_down


def solution(mesh):
    rows = P(("dom", "blk", "sub", "rep"), None)
    weights = P("sub", "rep", "blk")
    grads = P(("dom", "sub"), "rep", "blk")
    return jax.shard_map(
        on_device,
        mesh=mesh,
        in_specs=(rows, rows, rows, weights, weights, weights, rows),
        out_specs=(rows, rows, rows, grads, grads, grads),
        check_vma=False,
    )
```

```python
import functools

import jax
import jax.numpy as jnp
from jax import lax
from jax.experimental import pallas as pl
from jax.experimental.pallas import tpu as pltpu
from jax.sharding import PartitionSpec as P

NUM_EXPERTS = 128
TOPK = 8
CAP = 12
VMEM_LIMIT = 60 << 20
MESH = pl.DeviceIdType.MESH
BF16 = jnp.bfloat16
F32 = jnp.float32


def each(low, high, body):
    if high - low <= 8:
        for i in range(low, high):
            body(i)
    else:

        def step(i, carry):
            body(i)
            return carry

        lax.fori_loop(low, high, step, 0)


def div_mod(k, n):
    if isinstance(k, int):
        return k // n, k % n
    return lax.div(k, n), lax.rem(k, n)


def steps_of(v, width, count):
    out = jnp.zeros_like(v)
    for m in range(1, count):
        out = out + (v >= m * width).astype(jnp.int32)
    return out


def dot(a, b):
    return jnp.dot(a, b, preferred_element_type=F32)


def dot_nt(a, b):
    return lax.dot_general(a, b, (((1,), (1,)), ((), ())), preferred_element_type=F32)


def dot_tn(a, b):
    return lax.dot_general(a, b, (((0,), (0,)), ((), ())), preferred_element_type=F32)


def as_mask(cond):
    return jnp.where(cond, 1.0, 0.0).astype(BF16)


def kernel(
    dims,
    ids_hbm,
    gw_hbm,
    tok_hbm,
    cot_hbm,
    wg_hbm,
    wu_hbm,
    wd_hbm,
    ids_ref,
    sel_ref,
    selw_ref,
    cots,
    xs,
    dos,
    hid,
    back,
    gw_ref,
    tok_ref,
    cot_ref,
    wg_ref,
    wu_ref,
    wd_ref,
    send1,
    recv1,
    part_own,
    part_send,
    part_recv,
    px_own,
    px_send,
    px_recv,
    fin,
    in_s,
    disp_s,
    disp_r,
    fwd_s,
    fwd_r,
    rs_s,
    rs_r,
    ag_s,
    ag_r,
    ag_l,
    px_s,
    px_r,
    bk_s,
    bk_r,
):
    n_blk, n_sub, n_rep, halves, pack = dims
    tok_count = tok_ref.shape[0]
    d_blk = wg_ref.shape[2]
    ff = wg_ref.shape[1]
    width = d_blk // halves
    per_blk = n_sub * n_rep
    chunk = per_blk * CAP
    rows = n_sub * pack
    kinds = 2 * halves
    pieces = hid.shape[1]
    unit = ff // pieces
    b = lax.axis_index("blk")
    s = lax.axis_index("sub")
    r = lax.axis_index("rep")
    other = 1 - r

    def wrap(v, n):
        return lax.rem(v + n, n)

    operands = (
        (ids_hbm, ids_ref),
        (gw_hbm, gw_ref),
        (tok_hbm, tok_ref),
        (cot_hbm, cot_ref),
        (wg_hbm, wg_ref),
        (wu_hbm, wu_ref),
        (wd_hbm, wd_ref),
    )
    fetches = [pltpu.make_async_copy(src, dst, in_s.at[i]) for i, (src, dst) in enumerate(operands)]
    for fetch in fetches:
        fetch.start()

    barrier = pltpu.get_barrier_semaphore()
    group = n_blk * n_sub * n_rep

    def greet(k):
        db, rest = div_mod(k, n_sub * n_rep)
        ds, dr = div_mod(rest, n_rep)
        pl.semaphore_signal(
            barrier,
            inc=1,
            device_id={"blk": wrap(b + db, n_blk), "sub": wrap(s + ds, n_sub), "rep": wrap(r + dr, n_rep)},
            device_id_type=MESH,
        )

    each(1, group, greet)

    for fetch in fetches[:2]:
        fetch.wait()

    sub_i = lax.broadcasted_iota(jnp.int32, (rows, tok_count), 0)
    sub_exp = steps_of(sub_i, pack, n_sub)
    sub_in = sub_i - sub_exp * pack
    sub_kind = steps_of(sub_in, CAP, kinds + 1)
    sub_slot = sub_in - sub_kind * CAP
    picked = jnp.zeros((rows, tok_count), F32)
    weight = jnp.zeros((rows, tok_count), F32)
    for k in range(ids_ref.shape[0]):
        hit = ids_ref[k : k + 1, :] == sub_exp
        picked = picked + jnp.where(hit, 1.0, 0.0)
        weight = weight + jnp.where(hit, gw_ref[k : k + 1, :], 0.0)
    row_i = lax.broadcasted_iota(jnp.int32, (tok_count, tok_count), 0)
    col_i = lax.broadcasted_iota(jnp.int32, (tok_count, tok_count), 1)
    before = dot(picked.astype(BF16), as_mask(row_i < col_i))
    placed = (before == sub_slot.astype(F32)) & (picked > 0.0) & (sub_kind < kinds)
    sel = jnp.where(placed, 1.0, 0.0)
    selw = jnp.where(placed, weight, 0.0)
    sel_ref[...] = sel
    selw_ref[...] = selw
    slot_gate = jnp.sum(selw, axis=1, keepdims=True)
    is_cot = sub_kind == 1
    for h in range(1, halves):
        is_cot = is_cot | (sub_kind == 2 * h + 1)
    row_scale = jnp.where(is_cot, jnp.broadcast_to(slot_gate, is_cot.shape), 1.0)[:, :1]
    takes = [jnp.where(sub_kind == x, sel, 0.0).astype(BF16) for x in range(kinds)]

    def columns(blk, h):
        return pl.ds(pl.multiple_of(blk * d_blk + h * width, width), width)

    my_q = b * per_blk + r * n_sub + s

    def disp_copy(k):
        db, ds = div_mod(k, n_sub)
        dst_b, dst_s = wrap(b + db, n_blk), wrap(s + ds, n_sub)
        return pltpu.make_async_remote_copy(
            src_ref=send1.at[dst_b, dst_s],
            dst_ref=recv1.at[my_q],
            send_sem=disp_s.at[k],
            recv_sem=disp_r.at[k],
            device_id={"blk": dst_b, "sub": dst_s},
            device_id_type=MESH,
        )

    def fwd_copy(k):
        db, ds = div_mod(k, n_sub)
        q = wrap(b - db, n_blk) * per_blk + r * n_sub + wrap(s - ds, n_sub)
        return pltpu.make_async_remote_copy(
            src_ref=recv1.at[q],
            dst_ref=recv1.at[q],
            send_sem=fwd_s.at[k],
            recv_sem=fwd_r.at[k],
            device_id={"rep": other},
            device_id_type=MESH,
        )

    def gather(db):
        blk = wrap(b + db, n_blk)
        acc = None
        for h in range(halves):
            cols = columns(blk, h)
            term = dot(takes[2 * h], tok_ref[:, cols]) + dot(takes[2 * h + 1], cot_ref[:, cols])
            acc = term if acc is None else acc + term
        send1[blk] = (acc * row_scale).astype(BF16).reshape(n_sub, pack, width)

    def send_rows(db):
        each(0, n_sub, lambda ds: disp_copy(db * n_sub + ds).start())

    for fetch in fetches[2:4]:
        fetch.wait()
    gather(1)
    pl.semaphore_wait(barrier, group - 1)
    send_rows(1)

    def gather_send(db):
        gather(db)
        send_rows(db)

    each(2, n_blk, gather_send)
    gather(0)
    each(1, n_sub, lambda ds: disp_copy(ds).start())
    recv1[my_q] = send1[b, s]
    fwd_copy(0).start()

    def forward(db):
        def one(ds):
            k = db * n_sub + ds
            disp_copy(k).wait_recv()
            fwd_copy(k).start()

        each(0, n_sub, one)

    def forward_first(ds):
        disp_copy(ds).wait_recv()
        fwd_copy(ds).start()

    each(1, n_sub, forward_first)

    prow = lax.broadcasted_iota(jnp.int32, (chunk, per_blk * pack), 0)
    pcol = lax.broadcasted_iota(jnp.int32, (chunk, per_blk * pack), 1)
    prow_g = steps_of(prow, CAP, per_blk)
    pcol_g = steps_of(pcol, pack, per_blk)
    prow_c = prow - prow_g * CAP
    pcol_j = pcol - pcol_g * pack
    unpack = [as_mask((prow_g == pcol_g) & (pcol_j == x * CAP + prow_c)) for x in range(kinds)]

    def cot_rows(db):
        blk = wrap(b + db, n_blk)
        acc = None
        for h in range(halves):
            term = dot(takes[2 * h], cot_ref[:, columns(blk, h)])
            acc = term if acc is None else acc + term
        cots[blk] = acc.astype(BF16)

    each(0, n_blk, cot_rows)

    def rs_copy(db, p):
        return pltpu.make_async_remote_copy(
            src_ref=part_send.at[db, p],
            dst_ref=part_recv.at[db, p],
            send_sem=rs_s.at[db * pieces + p],
            recv_sem=rs_r.at[db * pieces + p],
            device_id={"blk": wrap(b - db, n_blk)},
            device_id_type=MESH,
        )

    def partial(db):
        blk = wrap(b - db, n_blk)
        each(0, n_sub, lambda ds: fwd_copy(db * n_sub + ds).wait_recv())
        block = recv1[pl.ds(blk * per_blk, per_blk)].reshape(per_blk * pack, width)
        for h in range(halves):
            xs[blk, :, h * width : (h + 1) * width] = dot(unpack[2 * h], block).astype(BF16)
            dos[blk, :, h * width : (h + 1) * width] = dot(unpack[2 * h + 1], block).astype(BF16)
        x, do = xs[blk], dos[blk]
        return dot_nt(x, wg_ref[0]), dot_nt(x, wu_ref[0]), dot_nt(do, wd_ref[0])

    def partial_send(db):
        values = partial(db)
        for p in range(pieces):
            for m, value in enumerate(values):
                part_send[db, p, :, m * unit : (m + 1) * unit] = value[:, p * unit : (p + 1) * unit].astype(BF16)
            rs_copy(db, p).start()

    for fetch in fetches[4:]:
        fetch.wait()
    forward(1)
    for m, value in enumerate(partial(0)):
        for p in range(pieces):
            part_own[p, :, m * unit : (m + 1) * unit] = value[:, p * unit : (p + 1) * unit]

    def middle(db):
        forward(db + 1)
        partial_send(db)

    each(1, n_blk - 1, middle)
    partial_send(n_blk - 1)

    def ag_copy(c, p, to, sem):
        return pltpu.make_async_remote_copy(
            src_ref=hid.at[c, p],
            dst_ref=hid.at[c, p],
            send_sem=sem,
            recv_sem=ag_r.at[c * pieces + p],
            device_id={"blk": to},
            device_id_type=MESH,
        )

    def to_right(p):
        return ag_copy(b, p, wrap(b + 1, n_blk), ag_s.at[b * pieces + p])

    def to_left(p):
        return ag_copy(b, p, wrap(b - 1, n_blk), ag_l.at[p])

    def both_ways(p, act):
        @pl.when(b + 1 < n_blk)
        def _():
            act(to_right(p))

        @pl.when(b >= 1)
        def _():
            act(to_left(p))

    for p in range(pieces):

        def add_part(db):
            rs_copy(db, p).wait_recv()
            part_own[p] += part_recv[db, p].astype(F32)

        each(1, n_blk, add_part)
        pre_gate = part_own[p, :, :unit]
        pre_up = part_own[p, :, unit : 2 * unit]
        dhid = part_own[p, :, 2 * unit :]
        sig = jax.nn.sigmoid(pre_gate)
        act = pre_gate * sig
        slope = sig * (1.0 + pre_gate * (1.0 - sig))
        hid[b, p, :, :unit] = (act * pre_up).astype(BF16)
        hid[b, p, :, unit : 2 * unit] = (dhid * pre_up * slope).astype(BF16)
        hid[b, p, :, 2 * unit :] = (dhid * act).astype(BF16)
        both_ways(p, lambda copy: copy.start())

    def pass_copy(c, p, step):
        return ag_copy(c, p, wrap(b + step, n_blk), ag_s.at[c * pieces + p])

    def onward(step):
        return (b + step >= 0) & (b + step < n_blk)

    def take(d):
        for p in range(pieces):

            def one(c, step):
                pass_copy(c, p, step).wait_recv()

                @pl.when(onward(step))
                def _():
                    pass_copy(c, p, step).start()

            at_distance(d, one)

    def passed(d):
        for p in range(pieces):

            def one(c, step):
                @pl.when(onward(step))
                def _():
                    pass_copy(c, p, step).wait_send()

            at_distance(d, one)

    def at_distance(d, fn):
        @pl.when(b - d >= 0)
        def _():
            fn(b - d, 1)

        @pl.when(b + d < n_blk)
        def _():
            fn(b + d, -1)

    srow = lax.broadcasted_iota(jnp.int32, (rows, chunk), 0)
    scol = lax.broadcasted_iota(jnp.int32, (rows, chunk), 1)
    srow_s = steps_of(srow, pack, n_sub)
    srow_j = srow - srow_s * pack
    srow_x = steps_of(srow_j, CAP, kinds + 1)
    srow_at = srow_s * CAP + srow_j - srow_x * CAP

    def repack(rep):
        at = scol == srow_at + rep * (n_sub * CAP)
        return [as_mask(at & (srow_x == x)) for x in range(kinds)]

    to_mine, to_other = repack(r), repack(other)

    def px_copy(c):
        return pltpu.make_async_remote_copy(
            src_ref=px_send.at[c],
            dst_ref=px_recv.at[c],
            send_sem=px_s.at[c],
            recv_sem=px_r.at[c],
            device_id={"rep": other},
            device_id_type=MESH,
        )

    def bk_copy(c, dst_s):
        return pltpu.make_async_remote_copy(
            src_ref=fin.at[c, dst_s],
            dst_ref=back.at[b, s],
            send_sem=bk_s.at[c * n_sub + dst_s],
            recv_sem=bk_r.at[b * n_sub + s],
            device_id={"blk": c, "sub": dst_s},
            device_id_type=MESH,
        )

    def bk_arrival(k):
        db, ds = div_mod(k, n_sub)
        from_b, from_s = wrap(b + db, n_blk), wrap(s + ds, n_sub)
        return pltpu.make_async_remote_copy(
            src_ref=fin.at[from_b, from_s],
            dst_ref=back.at[from_b, from_s],
            send_sem=bk_s.at[from_b * n_sub + from_s],
            recv_sem=bk_r.at[from_b * n_sub + from_s],
            device_id={"blk": from_b, "sub": from_s},
            device_id_type=MESH,
        )

    def outputs(c, step):
        def whole(m):
            return jnp.concatenate([hid[c, p, :, m * unit : (m + 1) * unit] for p in range(pieces)], axis=1)

        out = dot(whole(0), wd_ref[0]).astype(BF16)
        into = (dot(whole(1), wg_ref[0]) + dot(whole(2), wu_ref[0])).astype(BF16)

        def packed(masks):
            acc = None
            for h in range(halves):
                cols = slice(h * width, (h + 1) * width)
                term = dot(masks[2 * h], out[:, cols]) + dot(masks[2 * h + 1], into[:, cols])
                acc = term if acc is None else acc + term
            return acc.astype(BF16).reshape(n_sub, pack, width)

        px_send[c] = packed(to_other)
        px_copy(c).start()
        px_own[c] = packed(to_mine)

    def finish(c, step):
        px_copy(c).wait_recv()
        fin[c] = (px_own[c].astype(F32) + px_recv[c].astype(F32)).astype(BF16)
        each(0, n_sub, lambda dst_s: bk_copy(c, dst_s).start())

    outputs(b, 0)

    def near(d):
        take(d)
        take(d + 1)
        at_distance(d, outputs)
        at_distance(d + 1, outputs)
        at_distance(d, finish)
        at_distance(d + 1, finish)

    each(0, (n_blk - 1) // 2, lambda i: near(1 + 2 * i))
    if n_blk % 2 == 0:
        take(n_blk - 1)
        at_distance(n_blk - 1, outputs)
        at_distance(n_blk - 1, finish)
    px_copy(b).wait_recv()
    fin[b] = (px_own[b].astype(F32) + px_recv[b].astype(F32)).astype(BF16)
    each(1, n_sub, lambda ds: bk_copy(b, wrap(s + ds, n_sub)).start())
    back[b, s] = fin[b, s]
    each(1, n_blk * n_sub, lambda k: bk_arrival(k).wait_recv())

    each(1, n_blk * n_sub, lambda k: disp_copy(k).wait_send())
    each(0, n_blk * n_sub, lambda k: fwd_copy(k).wait_send())
    for p in range(pieces):
        each(1, n_blk, lambda db: rs_copy(db, p).wait_send())
        both_ways(p, lambda copy: copy.wait_send())
    each(1, n_blk, passed)
    each(0, n_blk, lambda c: px_copy(c).wait_send())
    each(1, n_blk * n_sub, lambda k: bk_arrival(k).wait_send())


def finish_kernel(
    dims,
    ids_hbm,
    sel_hbm,
    selw_hbm,
    cots_hbm,
    xs_hbm,
    dos_hbm,
    hid_hbm,
    back_hbm,
    mixed_hbm,
    tgrad_hbm,
    ggrad_hbm,
    gg_hbm,
    gu_hbm,
    gd_hbm,
    mixed_ref,
    tgrad_ref,
    ggrad_ref,
    gg_ref,
    gu_ref,
    gd_ref,
    ids_ref,
    sel_ref,
    selw_ref,
    cots,
    xs,
    dos,
    hid,
    back,
    sems,
    in_sems,
):
    n_blk, n_sub, halves, pack, scale = dims
    d_blk = xs.shape[2]
    all_rows = n_blk * xs.shape[1]
    pieces, unit = hid.shape[1], hid.shape[3] // 3
    width = d_blk // halves
    rows = n_sub * pack
    kinds = 2 * halves
    pairs = (
        (mixed_ref, mixed_hbm),
        (tgrad_ref, tgrad_hbm),
        (ggrad_ref, ggrad_hbm),
        (gg_ref, gg_hbm),
        (gu_ref, gu_hbm),
        (gd_ref, gd_hbm),
    )
    outs = [pltpu.make_async_copy(src, dst, sems.at[i]) for i, (src, dst) in enumerate(pairs)]
    operands = (
        (xs_hbm, xs),
        (hid_hbm, hid),
        (dos_hbm, dos),
        (ids_hbm, ids_ref),
        (sel_hbm, sel_ref),
        (selw_hbm, selw_ref),
        (cots_hbm, cots),
        (back_hbm, back),
    )
    fetches = [pltpu.make_async_copy(src, dst, in_sems.at[i]) for i, (src, dst) in enumerate(operands)]
    for fetch in fetches:
        fetch.start()
    for fetch in fetches[:3]:
        fetch.wait()
    x_all = xs[...].reshape(all_rows, d_blk)
    do_all = dos[...].reshape(all_rows, d_blk)

    def weight_grad(m, right, out_ref):
        for p in range(pieces):
            left = hid[:, p, :, m * unit : (m + 1) * unit].reshape(all_rows, unit)
            out_ref[0, p * unit : (p + 1) * unit, :] = dot_tn(left, right) * scale

    weight_grad(1, x_all, gg_ref)
    outs[3].start()
    weight_grad(2, x_all, gu_ref)
    outs[4].start()
    weight_grad(0, do_all, gd_ref)
    outs[5].start()

    for fetch in fetches[3:]:
        fetch.wait()
    tok_count = sel_ref.shape[1]
    sub_i = lax.broadcasted_iota(jnp.int32, (rows, tok_count), 0)
    sub_exp = steps_of(sub_i, pack, n_sub)
    sub_kind = steps_of(sub_i - sub_exp * pack, CAP, kinds + 1)
    selw = selw_ref[...]
    high = selw.astype(BF16).astype(F32)
    low = selw - high
    takes = []
    for h in range(halves):
        mine = sub_kind == 2 * h
        takes.append(
            [
                jnp.where(mine, high, 0.0).T.astype(BF16),
                jnp.where(mine, low, 0.0).T.astype(BF16),
                jnp.where(sub_kind == 2 * h + 1, sel_ref[...], 0.0).T.astype(BF16),
            ]
        )
    dots = jnp.zeros((rows, 1), F32)
    for blk in range(n_blk):
        got = back[blk].reshape(rows, width)
        for h in range(halves):
            cols = slice(blk * d_blk + h * width, blk * d_blk + (h + 1) * width)
            high_t, low_t, ones_t = takes[h]
            mixed_ref[:, cols] = (dot(high_t, got) + dot(low_t, got)).astype(BF16)
            tgrad_ref[:, cols] = dot(ones_t, got).astype(BF16)
        dots = dots + jnp.sum(cots[blk].astype(F32) * got.astype(F32), axis=1, keepdims=True)
    outs[0].start()
    outs[1].start()
    token_dots = sel_ref[...] * dots
    for k in range(ids_ref.shape[0]):
        hit = ids_ref[k : k + 1, :] == sub_exp
        ggrad_ref[k : k + 1, :] = jnp.sum(jnp.where(hit, token_dots, 0.0), axis=0, keepdims=True)
    outs[2].start()
    for out in outs:
        out.wait()


def on_device(tokens, expert_ids, gate_weights, w_gate, w_up, w_down, cotangent):
    n_blk, n_sub, n_rep = (lax.axis_size(name) for name in ("blk", "sub", "rep"))
    tok_count, d_model = tokens.shape
    _, ff, d_blk = w_gate.shape
    scale = (tok_count * n_blk * n_sub * n_rep * TOPK / NUM_EXPERTS) ** (-0.5)
    halves = 2 if d_blk % 256 == 0 else 1
    width = d_blk // halves
    pack = -(-2 * halves * CAP // 16) * 16
    rows = n_sub * pack
    chunk = n_sub * n_rep * CAP
    pairs = n_blk * n_sub
    dma = pltpu.SemaphoreType.DMA
    vmem = pl.BlockSpec(memory_space=pltpu.VMEM)
    anywhere = pl.BlockSpec(memory_space=pl.ANY)
    packed = (n_blk, n_sub, pack, width)
    shaped = jax.ShapeDtypeStruct
    pieces = ff // 128 if ff % 128 == 0 else 1
    spread = (n_blk, pieces, chunk, 3 * ff // pieces)
    ids, gates = expert_ids.T, gate_weights.T
    handed = (
        shaped(ids.shape, ids.dtype),
        shaped((rows, tok_count), F32),
        shaped((rows, tok_count), F32),
        shaped((n_blk, rows, width), BF16),
        shaped((n_blk, chunk, d_blk), BF16),
        shaped((n_blk, chunk, d_blk), BF16),
        shaped(spread, BF16),
        shaped(packed, BF16),
    )
    held = [
        (gates.shape, F32),
        (tokens.shape, BF16),
        (tokens.shape, BF16),
        ((1, ff, d_blk), BF16),
        ((1, ff, d_blk), BF16),
        ((1, ff, d_blk), BF16),
        (packed, BF16),
        ((pairs * n_rep, pack, width), BF16),
        (spread[1:], F32),
        (spread, BF16),
        (spread, BF16),
        (packed, BF16),
        (packed, BF16),
        (packed, BF16),
        (packed, BF16),
    ]
    between = pl.pallas_call(
        functools.partial(kernel, (n_blk, n_sub, n_rep, halves, pack)),
        out_shape=handed,
        in_specs=[pl.BlockSpec(memory_space=pltpu.HBM)] * 7,
        out_specs=(vmem,) * len(handed),
        scratch_shapes=[pltpu.VMEM(shape, kind) for shape, kind in held]
        + [dma((7,))]
        + [dma((pairs,))] * 4
        + [dma((n_blk * pieces,))] * 4
        + [dma((pieces,))]
        + [dma((n_blk,))] * 2
        + [dma((pairs,))] * 2,
        compiler_params=pltpu.CompilerParams(
            collective_id=0,
            has_side_effects=True,
            vmem_limit_bytes=VMEM_LIMIT,
        ),
        cost_estimate=pl.CostEstimate(flops=1 << 30, bytes_accessed=8 << 20, transcendentals=chunk * ff),
    )(ids, gates, tokens, cotangent, w_gate, w_up, w_down)
    grad = shaped((1, ff, d_blk), F32)
    results = (
        shaped((tok_count, d_model), BF16),
        shaped((tok_count, d_model), BF16),
        shaped(gates.shape, F32),
        grad,
        grad,
        grad,
    )
    mixed, token_grad, gate_grad, grad_gate, grad_up, grad_down = pl.pallas_call(
        functools.partial(finish_kernel, (n_blk, n_sub, halves, pack, scale)),
        out_shape=results,
        in_specs=[anywhere] * len(handed),
        out_specs=(anywhere,) * len(results),
        scratch_shapes=[pltpu.VMEM(one.shape, one.dtype) for one in results + handed]
        + [dma((len(results),)), dma((len(handed),))],
        compiler_params=pltpu.CompilerParams(vmem_limit_bytes=VMEM_LIMIT),
        cost_estimate=pl.CostEstimate(flops=1 << 28, bytes_accessed=5 << 20, transcendentals=0),
    )(*between)
    return mixed, token_grad, gate_grad.T, grad_gate, grad_up, grad_down


def solution(mesh):
    rows = P(("dom", "blk", "sub", "rep"), None)
    weights = P("sub", "rep", "blk")
    grads = P(("dom", "sub"), "rep", "blk")
    return jax.shard_map(
        on_device,
        mesh=mesh,
        in_specs=(rows, rows, rows, weights, weights, weights, rows),
        out_specs=(rows, rows, rows, grads, grads, grads),
        check_vma=False,
    )
```

```python
import functools

import jax
import jax.numpy as jnp
from jax import lax
from jax.experimental import pallas as pl
from jax.experimental.pallas import tpu as pltpu
from jax.sharding import PartitionSpec as P

NUM_EXPERTS = 128
TOPK = 8
CAP = 12
VMEM_LIMIT = 60 << 20
MESH = pl.DeviceIdType.MESH
BF16 = jnp.bfloat16
F32 = jnp.float32


def each(low, high, body):
    if high - low <= 8:
        for i in range(low, high):
            body(i)
    else:

        def step(i, carry):
            body(i)
            return carry

        lax.fori_loop(low, high, step, 0)


def div_mod(k, n):
    if isinstance(k, int):
        return k // n, k % n
    return lax.div(k, n), lax.rem(k, n)


def steps_of(v, width, count):
    out = jnp.zeros_like(v)
    for m in range(1, count):
        out = out + (v >= m * width).astype(jnp.int32)
    return out


def dot(a, b):
    return jnp.dot(a, b, preferred_element_type=F32)


def dot_nt(a, b):
    return lax.dot_general(a, b, (((1,), (1,)), ((), ())), preferred_element_type=F32)


def dot_tn(a, b):
    return lax.dot_general(a, b, (((0,), (0,)), ((), ())), preferred_element_type=F32)


def as_mask(cond):
    return jnp.where(cond, 1.0, 0.0).astype(BF16)


def kernel(
    dims,
    ids_hbm,
    gw_hbm,
    tok_hbm,
    cot_hbm,
    wg_hbm,
    wu_hbm,
    wd_hbm,
    ids_ref,
    sel_ref,
    selw_ref,
    cots,
    xs,
    dos,
    hid,
    back,
    gw_ref,
    tok_ref,
    cot_ref,
    wg_ref,
    wu_ref,
    wd_ref,
    send1,
    recv1,
    part_own,
    part_send,
    part_recv,
    px_own,
    px_send,
    px_recv,
    fin,
    in_s,
    disp_s,
    disp_r,
    fwd_s,
    fwd_r,
    rs_s,
    rs_r,
    ag_s,
    ag_r,
    ag_l,
    px_s,
    px_r,
    bk_s,
    bk_r,
):
    n_blk, n_sub, n_rep, halves, pack = dims
    tok_count = tok_ref.shape[0]
    d_blk = wg_ref.shape[2]
    ff = wg_ref.shape[1]
    width = d_blk // halves
    per_blk = n_sub * n_rep
    chunk = per_blk * CAP
    rows = n_sub * pack
    kinds = 2 * halves
    pieces = hid.shape[1]
    unit = ff // pieces
    b = lax.axis_index("blk")
    s = lax.axis_index("sub")
    r = lax.axis_index("rep")
    other = 1 - r

    def wrap(v, n):
        return lax.rem(v + n, n)

    operands = (
        (ids_hbm, ids_ref),
        (gw_hbm, gw_ref),
        (tok_hbm, tok_ref),
        (cot_hbm, cot_ref),
        (wg_hbm, wg_ref),
        (wu_hbm, wu_ref),
        (wd_hbm, wd_ref),
    )
    fetches = [pltpu.make_async_copy(src, dst, in_s.at[i]) for i, (src, dst) in enumerate(operands)]
    for fetch in fetches:
        fetch.start()

    barrier = pltpu.get_barrier_semaphore()
    group = n_blk * n_sub * n_rep

    def greet(k):
        db, rest = div_mod(k, n_sub * n_rep)
        ds, dr = div_mod(rest, n_rep)
        pl.semaphore_signal(
            barrier,
            inc=1,
            device_id={"blk": wrap(b + db, n_blk), "sub": wrap(s + ds, n_sub), "rep": wrap(r + dr, n_rep)},
            device_id_type=MESH,
        )

    each(1, group, greet)

    for fetch in fetches[:2]:
        fetch.wait()

    sub_i = lax.broadcasted_iota(jnp.int32, (rows, tok_count), 0)
    sub_exp = steps_of(sub_i, pack, n_sub)
    sub_in = sub_i - sub_exp * pack
    sub_kind = steps_of(sub_in, CAP, kinds + 1)
    sub_slot = sub_in - sub_kind * CAP
    picked = jnp.zeros((rows, tok_count), F32)
    weight = jnp.zeros((rows, tok_count), F32)
    for k in range(ids_ref.shape[0]):
        hit = ids_ref[k : k + 1, :] == sub_exp
        picked = picked + jnp.where(hit, 1.0, 0.0)
        weight = weight + jnp.where(hit, gw_ref[k : k + 1, :], 0.0)
    row_i = lax.broadcasted_iota(jnp.int32, (tok_count, tok_count), 0)
    col_i = lax.broadcasted_iota(jnp.int32, (tok_count, tok_count), 1)
    before = dot(picked.astype(BF16), as_mask(row_i < col_i))
    placed = (before == sub_slot.astype(F32)) & (picked > 0.0) & (sub_kind < kinds)
    sel = jnp.where(placed, 1.0, 0.0)
    selw = jnp.where(placed, weight, 0.0)
    sel_ref[...] = sel
    selw_ref[...] = selw
    slot_gate = jnp.sum(selw, axis=1, keepdims=True)
    is_cot = sub_kind == 1
    for h in range(1, halves):
        is_cot = is_cot | (sub_kind == 2 * h + 1)
    row_scale = jnp.where(is_cot, jnp.broadcast_to(slot_gate, is_cot.shape), 1.0)[:, :1]
    takes = [jnp.where(sub_kind == x, sel, 0.0).astype(BF16) for x in range(kinds)]

    def columns(blk, h):
        return pl.ds(pl.multiple_of(blk * d_blk + h * width, width), width)

    my_q = b * per_blk + r * n_sub + s

    def disp_copy(k):
        db, ds = div_mod(k, n_sub)
        dst_b, dst_s = wrap(b + db, n_blk), wrap(s + ds, n_sub)
        return pltpu.make_async_remote_copy(
            src_ref=send1.at[dst_b, dst_s],
            dst_ref=recv1.at[my_q],
            send_sem=disp_s.at[k],
            recv_sem=disp_r.at[k],
            device_id={"blk": dst_b, "sub": dst_s},
            device_id_type=MESH,
        )

    def fwd_copy(k):
        db, ds = div_mod(k, n_sub)
        q = wrap(b - db, n_blk) * per_blk + r * n_sub + wrap(s - ds, n_sub)
        return pltpu.make_async_remote_copy(
            src_ref=recv1.at[q],
            dst_ref=recv1.at[q],
            send_sem=fwd_s.at[k],
            recv_sem=fwd_r.at[k],
            device_id={"rep": other},
            device_id_type=MESH,
        )

    def gather(db):
        blk = wrap(b + db, n_blk)
        acc = None
        for h in range(halves):
            cols = columns(blk, h)
            term = dot(takes[2 * h], tok_ref[:, cols]) + dot(takes[2 * h + 1], cot_ref[:, cols])
            acc = term if acc is None else acc + term
        send1[blk] = (acc * row_scale).astype(BF16).reshape(n_sub, pack, width)

    def send_rows(db):
        each(0, n_sub, lambda ds: disp_copy(db * n_sub + ds).start())

    for fetch in fetches[2:4]:
        fetch.wait()
    gather(1)
    pl.semaphore_wait(barrier, group - 1)
    send_rows(1)

    def gather_send(db):
        gather(db)
        send_rows(db)

    each(2, n_blk, gather_send)
    gather(0)
    each(1, n_sub, lambda ds: disp_copy(ds).start())
    recv1[my_q] = send1[b, s]
    fwd_copy(0).start()

    def forward(db):
        def one(ds):
            k = db * n_sub + ds
            disp_copy(k).wait_recv()
            fwd_copy(k).start()

        each(0, n_sub, one)

    def forward_first(ds):
        disp_copy(ds).wait_recv()
        fwd_copy(ds).start()

    each(1, n_sub, forward_first)

    prow = lax.broadcasted_iota(jnp.int32, (chunk, per_blk * pack), 0)
    pcol = lax.broadcasted_iota(jnp.int32, (chunk, per_blk * pack), 1)
    prow_g = steps_of(prow, CAP, per_blk)
    pcol_g = steps_of(pcol, pack, per_blk)
    prow_c = prow - prow_g * CAP
    pcol_j = pcol - pcol_g * pack
    unpack = [as_mask((prow_g == pcol_g) & (pcol_j == x * CAP + prow_c)) for x in range(kinds)]

    def cot_rows(db):
        blk = wrap(b + db, n_blk)
        acc = None
        for h in range(halves):
            term = dot(takes[2 * h], cot_ref[:, columns(blk, h)])
            acc = term if acc is None else acc + term
        cots[blk] = acc.astype(BF16)

    def rs_copy(db, p):
        return pltpu.make_async_remote_copy(
            src_ref=part_send.at[db, p],
            dst_ref=part_recv.at[db, p],
            send_sem=rs_s.at[db * pieces + p],
            recv_sem=rs_r.at[db * pieces + p],
            device_id={"blk": wrap(b - db, n_blk)},
            device_id_type=MESH,
        )

    def partial(db):
        blk = wrap(b - db, n_blk)
        each(0, n_sub, lambda ds: fwd_copy(db * n_sub + ds).wait_recv())
        block = recv1[pl.ds(blk * per_blk, per_blk)].reshape(per_blk * pack, width)
        for h in range(halves):
            xs[blk, :, h * width : (h + 1) * width] = dot(unpack[2 * h], block).astype(BF16)
            dos[blk, :, h * width : (h + 1) * width] = dot(unpack[2 * h + 1], block).astype(BF16)
        x, do = xs[blk], dos[blk]
        return dot_nt(x, wg_ref[0]), dot_nt(x, wu_ref[0]), dot_nt(do, wd_ref[0])

    def partial_send(db):
        values = partial(db)
        for p in range(pieces):
            for m, value in enumerate(values):
                part_send[db, p, :, m * unit : (m + 1) * unit] = value[:, p * unit : (p + 1) * unit].astype(BF16)
            rs_copy(db, p).start()

    for fetch in fetches[4:]:
        fetch.wait()
    forward(1)
    for m, value in enumerate(partial(0)):
        for p in range(pieces):
            part_own[p, :, m * unit : (m + 1) * unit] = value[:, p * unit : (p + 1) * unit]

    def middle(db):
        forward(db + 1)
        partial_send(db)

    each(1, n_blk - 1, middle)
    partial_send(n_blk - 1)

    def ag_copy(c, p, to, sem):
        return pltpu.make_async_remote_copy(
            src_ref=hid.at[c, p],
            dst_ref=hid.at[c, p],
            send_sem=sem,
            recv_sem=ag_r.at[c * pieces + p],
            device_id={"blk": to},
            device_id_type=MESH,
        )

    def to_right(p):
        return ag_copy(b, p, wrap(b + 1, n_blk), ag_s.at[b * pieces + p])

    def to_left(p):
        return ag_copy(b, p, wrap(b - 1, n_blk), ag_l.at[p])

    def both_ways(p, act):
        @pl.when(b + 1 < n_blk)
        def _():
            act(to_right(p))

        @pl.when(b >= 1)
        def _():
            act(to_left(p))

    for p in range(pieces):

        def add_part(db):
            rs_copy(db, p).wait_recv()
            part_own[p] += part_recv[db, p].astype(F32)

        each(1, n_blk, add_part)
        pre_gate = part_own[p, :, :unit]
        pre_up = part_own[p, :, unit : 2 * unit]
        dhid = part_own[p, :, 2 * unit :]
        sig = jax.nn.sigmoid(pre_gate)
        act = pre_gate * sig
        slope = sig * (1.0 + pre_gate * (1.0 - sig))
        hid[b, p, :, :unit] = (act * pre_up).astype(BF16)
        hid[b, p, :, unit : 2 * unit] = (dhid * pre_up * slope).astype(BF16)
        hid[b, p, :, 2 * unit :] = (dhid * act).astype(BF16)
        both_ways(p, lambda copy: copy.start())

    def pass_copy(c, p, step):
        return ag_copy(c, p, wrap(b + step, n_blk), ag_s.at[c * pieces + p])

    def onward(step):
        return (b + step >= 0) & (b + step < n_blk)

    def take(d):
        for p in range(pieces):

            def one(c, step):
                pass_copy(c, p, step).wait_recv()

                @pl.when(onward(step))
                def _():
                    pass_copy(c, p, step).start()

            at_distance(d, one)

    def passed(d):
        for p in range(pieces):

            def one(c, step):
                @pl.when(onward(step))
                def _():
                    pass_copy(c, p, step).wait_send()

            at_distance(d, one)

    def at_distance(d, fn):
        @pl.when(b - d >= 0)
        def _():
            fn(b - d, 1)

        @pl.when(b + d < n_blk)
        def _():
            fn(b + d, -1)

    srow = lax.broadcasted_iota(jnp.int32, (rows, chunk), 0)
    scol = lax.broadcasted_iota(jnp.int32, (rows, chunk), 1)
    srow_s = steps_of(srow, pack, n_sub)
    srow_j = srow - srow_s * pack
    srow_x = steps_of(srow_j, CAP, kinds + 1)
    srow_at = srow_s * CAP + srow_j - srow_x * CAP

    def repack(rep):
        at = scol == srow_at + rep * (n_sub * CAP)
        return [as_mask(at & (srow_x == x)) for x in range(kinds)]

    to_mine, to_other = repack(r), repack(other)

    def px_copy(c):
        return pltpu.make_async_remote_copy(
            src_ref=px_send.at[c],
            dst_ref=px_recv.at[c],
            send_sem=px_s.at[c],
            recv_sem=px_r.at[c],
            device_id={"rep": other},
            device_id_type=MESH,
        )

    def bk_copy(c, dst_s):
        return pltpu.make_async_remote_copy(
            src_ref=fin.at[c, dst_s],
            dst_ref=back.at[b, s],
            send_sem=bk_s.at[c * n_sub + dst_s],
            recv_sem=bk_r.at[b * n_sub + s],
            device_id={"blk": c, "sub": dst_s},
            device_id_type=MESH,
        )

    def bk_arrival(k):
        db, ds = div_mod(k, n_sub)
        from_b, from_s = wrap(b + db, n_blk), wrap(s + ds, n_sub)
        return pltpu.make_async_remote_copy(
            src_ref=fin.at[from_b, from_s],
            dst_ref=back.at[from_b, from_s],
            send_sem=bk_s.at[from_b * n_sub + from_s],
            recv_sem=bk_r.at[from_b * n_sub + from_s],
            device_id={"blk": from_b, "sub": from_s},
            device_id_type=MESH,
        )

    def outputs(c, step):
        def whole(m):
            return jnp.concatenate([hid[c, p, :, m * unit : (m + 1) * unit] for p in range(pieces)], axis=1)

        out = dot(whole(0), wd_ref[0]).astype(BF16)
        into = (dot(whole(1), wg_ref[0]) + dot(whole(2), wu_ref[0])).astype(BF16)

        def packed(masks):
            acc = None
            for h in range(halves):
                cols = slice(h * width, (h + 1) * width)
                term = dot(masks[2 * h], out[:, cols]) + dot(masks[2 * h + 1], into[:, cols])
                acc = term if acc is None else acc + term
            return acc.astype(BF16).reshape(n_sub, pack, width)

        px_send[c] = packed(to_other)
        px_copy(c).start()
        px_own[c] = packed(to_mine)

    def finish(c, step):
        px_copy(c).wait_recv()
        fin[c] = (px_own[c].astype(F32) + px_recv[c].astype(F32)).astype(BF16)
        each(0, n_sub, lambda dst_s: bk_copy(c, dst_s).start())

    outputs(b, 0)
    each(0, n_blk, cot_rows)

    def near(d):
        take(d)
        take(d + 1)
        at_distance(d, outputs)
        at_distance(d + 1, outputs)
        at_distance(d, finish)
        at_distance(d + 1, finish)

    each(0, (n_blk - 1) // 2, lambda i: near(1 + 2 * i))
    if n_blk % 2 == 0:
        take(n_blk - 1)
        at_distance(n_blk - 1, outputs)
        at_distance(n_blk - 1, finish)
    px_copy(b).wait_recv()
    fin[b] = (px_own[b].astype(F32) + px_recv[b].astype(F32)).astype(BF16)
    each(1, n_sub, lambda ds: bk_copy(b, wrap(s + ds, n_sub)).start())
    back[b, s] = fin[b, s]
    each(1, n_blk * n_sub, lambda k: bk_arrival(k).wait_recv())

    each(1, n_blk * n_sub, lambda k: disp_copy(k).wait_send())
    each(0, n_blk * n_sub, lambda k: fwd_copy(k).wait_send())
    for p in range(pieces):
        each(1, n_blk, lambda db: rs_copy(db, p).wait_send())
        both_ways(p, lambda copy: copy.wait_send())
    each(1, n_blk, passed)
    each(0, n_blk, lambda c: px_copy(c).wait_send())
    each(1, n_blk * n_sub, lambda k: bk_arrival(k).wait_send())


def finish_kernel(
    dims,
    ids_hbm,
    sel_hbm,
    selw_hbm,
    cots_hbm,
    xs_hbm,
    dos_hbm,
    hid_hbm,
    back_hbm,
    mixed_hbm,
    tgrad_hbm,
    ggrad_hbm,
    gg_hbm,
    gu_hbm,
    gd_hbm,
    mixed_ref,
    tgrad_ref,
    ggrad_ref,
    gg_ref,
    gu_ref,
    gd_ref,
    ids_ref,
    sel_ref,
    selw_ref,
    cots,
    xs,
    dos,
    hid,
    back,
    sems,
    in_sems,
):
    n_blk, n_sub, halves, pack, scale = dims
    d_blk = xs.shape[2]
    all_rows = n_blk * xs.shape[1]
    pieces, unit = hid.shape[1], hid.shape[3] // 3
    width = d_blk // halves
    rows = n_sub * pack
    kinds = 2 * halves
    pairs = (
        (mixed_ref, mixed_hbm),
        (tgrad_ref, tgrad_hbm),
        (ggrad_ref, ggrad_hbm),
        (gg_ref, gg_hbm),
        (gu_ref, gu_hbm),
        (gd_ref, gd_hbm),
    )
    outs = [pltpu.make_async_copy(src, dst, sems.at[i]) for i, (src, dst) in enumerate(pairs)]
    operands = (
        (xs_hbm, xs),
        (hid_hbm, hid),
        (dos_hbm, dos),
        (ids_hbm, ids_ref),
        (sel_hbm, sel_ref),
        (selw_hbm, selw_ref),
        (cots_hbm, cots),
        (back_hbm, back),
    )
    fetches = [pltpu.make_async_copy(src, dst, in_sems.at[i]) for i, (src, dst) in enumerate(operands)]
    for fetch in fetches:
        fetch.start()
    for fetch in fetches[:3]:
        fetch.wait()
    x_all = xs[...].reshape(all_rows, d_blk)
    do_all = dos[...].reshape(all_rows, d_blk)

    def weight_grad(m, right, out_ref):
        for p in range(pieces):
            left = hid[:, p, :, m * unit : (m + 1) * unit].reshape(all_rows, unit)
            out_ref[0, p * unit : (p + 1) * unit, :] = dot_tn(left, right) * scale

    weight_grad(1, x_all, gg_ref)
    outs[3].start()
    weight_grad(2, x_all, gu_ref)
    outs[4].start()
    weight_grad(0, do_all, gd_ref)
    outs[5].start()

    for fetch in fetches[3:]:
        fetch.wait()
    tok_count = sel_ref.shape[1]
    sub_i = lax.broadcasted_iota(jnp.int32, (rows, tok_count), 0)
    sub_exp = steps_of(sub_i, pack, n_sub)
    sub_kind = steps_of(sub_i - sub_exp * pack, CAP, kinds + 1)
    selw = selw_ref[...]
    high = selw.astype(BF16).astype(F32)
    low = selw - high
    takes = []
    for h in range(halves):
        mine = sub_kind == 2 * h
        takes.append(
            [
                jnp.where(mine, high, 0.0).T.astype(BF16),
                jnp.where(mine, low, 0.0).T.astype(BF16),
                jnp.where(sub_kind == 2 * h + 1, sel_ref[...], 0.0).T.astype(BF16),
            ]
        )
    dots = jnp.zeros((rows, 1), F32)
    for blk in range(n_blk):
        got = back[blk].reshape(rows, width)
        for h in range(halves):
            cols = slice(blk * d_blk + h * width, blk * d_blk + (h + 1) * width)
            high_t, low_t, ones_t = takes[h]
            mixed_ref[:, cols] = (dot(high_t, got) + dot(low_t, got)).astype(BF16)
            tgrad_ref[:, cols] = dot(ones_t, got).astype(BF16)
        dots = dots + jnp.sum(cots[blk].astype(F32) * got.astype(F32), axis=1, keepdims=True)
    outs[0].start()
    outs[1].start()
    token_dots = sel_ref[...] * dots
    for k in range(ids_ref.shape[0]):
        hit = ids_ref[k : k + 1, :] == sub_exp
        ggrad_ref[k : k + 1, :] = jnp.sum(jnp.where(hit, token_dots, 0.0), axis=0, keepdims=True)
    outs[2].start()
    for out in outs:
        out.wait()


def on_device(tokens, expert_ids, gate_weights, w_gate, w_up, w_down, cotangent):
    n_blk, n_sub, n_rep = (lax.axis_size(name) for name in ("blk", "sub", "rep"))
    tok_count, d_model = tokens.shape
    _, ff, d_blk = w_gate.shape
    scale = (tok_count * n_blk * n_sub * n_rep * TOPK / NUM_EXPERTS) ** (-0.5)
    halves = 2 if d_blk % 256 == 0 else 1
    width = d_blk // halves
    pack = -(-2 * halves * CAP // 16) * 16
    rows = n_sub * pack
    chunk = n_sub * n_rep * CAP
    pairs = n_blk * n_sub
    dma = pltpu.SemaphoreType.DMA
    vmem = pl.BlockSpec(memory_space=pltpu.VMEM)
    anywhere = pl.BlockSpec(memory_space=pl.ANY)
    packed = (n_blk, n_sub, pack, width)
    shaped = jax.ShapeDtypeStruct
    pieces = ff // 128 if ff % 128 == 0 else 1
    spread = (n_blk, pieces, chunk, 3 * ff // pieces)
    ids, gates = expert_ids.T, gate_weights.T
    handed = (
        shaped(ids.shape, ids.dtype),
        shaped((rows, tok_count), F32),
        shaped((rows, tok_count), F32),
        shaped((n_blk, rows, width), BF16),
        shaped((n_blk, chunk, d_blk), BF16),
        shaped((n_blk, chunk, d_blk), BF16),
        shaped(spread, BF16),
        shaped(packed, BF16),
    )
    held = [
        (gates.shape, F32),
        (tokens.shape, BF16),
        (tokens.shape, BF16),
        ((1, ff, d_blk), BF16),
        ((1, ff, d_blk), BF16),
        ((1, ff, d_blk), BF16),
        (packed, BF16),
        ((pairs * n_rep, pack, width), BF16),
        (spread[1:], F32),
        (spread, BF16),
        (spread, BF16),
        (packed, BF16),
        (packed, BF16),
        (packed, BF16),
        (packed, BF16),
    ]
    between = pl.pallas_call(
        functools.partial(kernel, (n_blk, n_sub, n_rep, halves, pack)),
        out_shape=handed,
        in_specs=[pl.BlockSpec(memory_space=pltpu.HBM)] * 7,
        out_specs=(vmem,) * len(handed),
        scratch_shapes=[pltpu.VMEM(shape, kind) for shape, kind in held]
        + [dma((7,))]
        + [dma((pairs,))] * 4
        + [dma((n_blk * pieces,))] * 4
        + [dma((pieces,))]
        + [dma((n_blk,))] * 2
        + [dma((pairs,))] * 2,
        compiler_params=pltpu.CompilerParams(
            collective_id=0,
            has_side_effects=True,
            vmem_limit_bytes=VMEM_LIMIT,
        ),
        cost_estimate=pl.CostEstimate(flops=1 << 30, bytes_accessed=8 << 20, transcendentals=chunk * ff),
    )(ids, gates, tokens, cotangent, w_gate, w_up, w_down)
    grad = shaped((1, ff, d_blk), F32)
    results = (
        shaped((tok_count, d_model), BF16),
        shaped((tok_count, d_model), BF16),
        shaped(gates.shape, F32),
        grad,
        grad,
        grad,
    )
    mixed, token_grad, gate_grad, grad_gate, grad_up, grad_down = pl.pallas_call(
        functools.partial(finish_kernel, (n_blk, n_sub, halves, pack, scale)),
        out_shape=results,
        in_specs=[anywhere] * len(handed),
        out_specs=(anywhere,) * len(results),
        scratch_shapes=[pltpu.VMEM(one.shape, one.dtype) for one in results + handed]
        + [dma((len(results),)), dma((len(handed),))],
        compiler_params=pltpu.CompilerParams(vmem_limit_bytes=VMEM_LIMIT),
        cost_estimate=pl.CostEstimate(flops=1 << 28, bytes_accessed=5 << 20, transcendentals=0),
    )(*between)
    return mixed, token_grad, gate_grad.T, grad_gate, grad_up, grad_down


def solution(mesh):
    rows = P(("dom", "blk", "sub", "rep"), None)
    weights = P("sub", "rep", "blk")
    grads = P(("dom", "sub"), "rep", "blk")
    return jax.shard_map(
        on_device,
        mesh=mesh,
        in_specs=(rows, rows, rows, weights, weights, weights, rows),
        out_specs=(rows, rows, rows, grads, grads, grads),
        check_vma=False,
    )
```
